32 devices in a mesh: grp: 16 (over z, x, core), freq: 2 (over y).
Axes of the slice: x: 2, y: 2, z: 4, core: 2. Of those that a mesh axis runs over, the one named last changes fastest.
Arguments:
- spectra: bfloat16 [2, 4096, 1024], P('freq', 'grp'), may hold values from -3000 to 3000
- valid: int32 [4096, 512], P('grp'), may hold values 0 or 1
- station_index: int32 [16], replicated, may hold values from 0 to 4095, as said below
Outputs:
- cross: bfloat16 [2, 2, 4096, 4096], P('freq', None, 'grp')
- station_gather: float32 [16, 4096, 256], P(None, 'grp', 'freq')
The draws below stay inside these ranges and needn't reach their ends.
Inputs may be any that keep to these rules, and one draw needn't show every extreme that they name: `station_index`: 16 distinct channel numbers.
All inputs are finite; a program needn't handle non-finite values. No bound on the sum of `valid` on one device may be relied on, other than what follows from the above.
Results may differ from the reference program's by a relative error of at most 0.0056.
Values may be sent and summed in bfloat16 or wider, within the bound.
No kernel may reach another device: no remote copies, remote signals or barrier semaphores. Data moves between devices by JAX's collectives and lax.ppermute only.
A program may use at most 128 MiB of HBM per device.

```python
import math
import jax
import jax.numpy as jnp
from jax import lax

WINDOWS = 512
STATIONS = 16
LAGS = 256
BINS = 2
CHANNELS = 4096


def draw_spectra(key, part):
    keys = jax.random.split(key, 4)
    shape = (BINS, CHANNELS, 2 * WINDOWS)
    base = jnp.clip(jax.random.normal(keys[0], shape, jnp.float32), -6.0, 6.0)
    bin_axis = jnp.arange(BINS).astype(jnp.float32)
    rise = jnp.exp(math.log(3.0) * bin_axis / max(BINS - 1, 1))
    jitter = jnp.exp(jax.random.uniform(keys[1], (BINS,), jnp.float32, -0.5, 0.5))
    channel_scale = jnp.exp(jax.random.uniform(keys[2], (CHANNELS,), jnp.float32, 0.0, math.log(10.0)))
    window_scale = jnp.exp(jax.random.uniform(keys[3], (WINDOWS,), jnp.float32, 0.0, math.log(10.0)))
    window_both = jnp.concatenate([window_scale, window_scale])
    values = base * (rise * jitter)[:, None, None] * channel_scale[None, :, None] * window_both[None, None, :]
    return values.astype(jnp.bfloat16)


def draw_station_index(key, part):
    order = jax.random.permutation(jax.random.fold_in(key, 7), CHANNELS)
    return order[:STATIONS].astype(jnp.int32)


def touch_ends(values, own_key, low, largest):
    longest = values.shape.index(max(values.shape))
    spots = []
    for shift in (0, 1):
        where = [jax.random.randint(jax.random.fold_in(own_key, axis), (), 0, length) for axis, length in enumerate(values.shape)]
        where[longest] = (where[longest] + shift) % values.shape[longest]
        spots.append(tuple(where))
    return values.at[spots[0]].set(low).at[spots[1]].set(largest)


def setup_inputs(seed: int = 0) -> dict:
    splits = jax.random.split(jax.random.key(seed), 4)
    spectra = draw_spectra(jax.random.fold_in(splits[3], 71), 0)
    valid = touch_ends((jax.random.randint(splits[1], (CHANNELS, WINDOWS), 0, 8) < 7).astype(jnp.int32), jax.random.fold_in(splits[1], 1), 0, 1)
    station_index = draw_station_index(jax.random.fold_in(splits[3], 71), 0)
    return {"spectra": spectra, "valid": valid, "station_index": station_index}


def reference(spectra, valid, station_index):
    spectrum_f32 = spectra.astype(jnp.float32)
    real_part = spectrum_f32[..., :WINDOWS]
    imag_part = spectrum_f32[..., WINDOWS:]
    band_power = lax.optimization_barrier(jnp.sum(real_part * real_part + imag_part * imag_part, axis=0))
    factor = lax.rsqrt(band_power / BINS + 1e-05) * valid.astype(jnp.float32)
    whitened = (spectrum_f32 * jnp.concatenate([factor, factor], axis=1)[None]).astype(jnp.bfloat16)
    swapped = jnp.concatenate([whitened[..., WINDOWS:], -whitened[..., :WINDOWS]], axis=2)
    stacked = jnp.concatenate([whitened, swapped], axis=1)
    scaling = 1.0 / math.sqrt(WINDOWS)

    def one_bin(operands):
        left_rows, right_rows = operands
        product = jnp.dot(left_rows, right_rows.T, preferred_element_type=jnp.float32)
        return (product * scaling).astype(jnp.bfloat16).reshape(2, CHANNELS, CHANNELS)
    cross = lax.map(one_bin, (stacked, whitened))
    station_left = jnp.concatenate([whitened[:, station_index], swapped[:, station_index]], axis=1)
    kernel = jnp.einsum('fkw,fjw->fkj', station_left.astype(jnp.float32), whitened.astype(jnp.float32), precision=lax.Precision.HIGHEST) * scaling
    kernel = kernel.reshape(BINS, 2, STATIONS, CHANNELS)
    bin_values = jnp.arange(BINS).astype(jnp.float32) + 1.0
    lag_values = jnp.arange(LAGS).astype(jnp.float32)
    phase = math.pi * bin_values[:, None] * lag_values[None, :] / LAGS
    lag_table = jnp.stack([jnp.cos(phase), -jnp.sin(phase)], axis=1)
    station_gather = jnp.einsum('frsc,frl->scl', kernel, lag_table, precision=lax.Precision.HIGHEST) / math.sqrt(BINS)
    return (cross, station_gather)
```

```python
import math

import jax
import jax.numpy as jnp
from jax import lax
from jax.experimental import pallas as pl
from jax.experimental.pallas import tpu as pltpu
from jax.sharding import PartitionSpec as P

LAGS = 256
ROWS_T = (((1,), (1,)), ((), ()))


def ring_pairs(group_size):
    chips = group_size // 2
    half = chips // 2

    def device(place, core):
        place %= chips
        z, x = (place, 0) if place < half else (chips - 1 - place, 1)
        return z * 4 + x * 2 + core

    pairs = []
    for place in range(chips):
        pairs.append((device(place, 0), device(place + 1, 0)))
        pairs.append((device(place, 1), device(place - 1, 1)))
    return pairs


def block_of(place, core, chips):
    place = lax.rem(place + chips, chips)
    half = chips // 2
    return jnp.where(place < half, place * 4, (chips - 1 - place) * 4 + 2) + core


def cross_kernel(scaling, first, where, left, one, two, *rest):
    out = rest[-3] if first else rest[1]
    held, sems = rest[-2:]
    copies = []
    for k, block in enumerate((one, two)):
        product = lax.dot_general(left[...], block[...], ROWS_T, preferred_element_type=jnp.float32)
        rows, width = block.shape[0], block.shape[0]
        held[k] = (product * scaling).astype(jnp.bfloat16).reshape(2, rows, width)
        start = pl.multiple_of(where[k] * width, width)
        copy = pltpu.make_async_copy(held.at[k], out.at[:, :, pl.ds(start, width)], sems.at[k])
        copy.start()
        copies.append(copy)
    for copy in copies:
        copy.wait()


def cross_blocks(left, one, two, where, cross, total, scaling):
    rows, depth = one.shape
    shape = jax.ShapeDtypeStruct((2, rows, total), jnp.bfloat16)
    first = cross is None
    vmem = pl.BlockSpec(memory_space=pltpu.VMEM)
    specs = [pl.BlockSpec(memory_space=pltpu.SMEM), vmem, vmem, vmem]
    args = [where, left, one, two]
    if not first:
        specs.append(pl.BlockSpec(memory_space=pl.ANY))
        args.append(cross)

    def body(*refs):
        cross_kernel(scaling, first, *refs)

    return pl.pallas_call(
        body,
        out_shape=shape,
        in_specs=specs,
        out_specs=pl.BlockSpec(memory_space=pl.ANY),
        scratch_shapes=[pltpu.VMEM((2, 2, rows, rows), jnp.bfloat16), pltpu.SemaphoreType.DMA((2,))],
        input_output_aliases={} if first else {4: 0},
        compiler_params=pltpu.CompilerParams(vmem_limit_bytes=16 * 2**20),
        cost_estimate=pl.CostEstimate(flops=4 * 2 * rows * rows * depth, bytes_accessed=4 * 2 * rows * depth, transcendentals=0),
    )(*args)


def make_on_device(group_size, freq_size):
    chips = group_size // 2
    ring = ring_pairs(group_size)

    def swap_by(bit):
        return [(g, g ^ bit) for g in range(group_size)]

    def from_freq(shift):
        return [(f, (f + shift) % freq_size) for f in range(freq_size)]

    def on_device(spectra, valid, station_index):
        bin_count, chan_count, double_width = spectra.shape
        assert bin_count == 1
        window_count = double_width // 2
        group_index = lax.axis_index("grp")
        freq_index = lax.axis_index("freq")
        core = lax.rem(group_index, 2)
        total_chans = chan_count * group_size
        total_bins = bin_count * freq_size
        scaling = 1.0 / math.sqrt(window_count)

        spectrum_f32 = spectra[0].astype(jnp.float32)
        real_part = spectrum_f32[:, :window_count]
        imag_part = spectrum_f32[:, window_count:]
        local_power = real_part * real_part + imag_part * imag_part
        sent_power = local_power.astype(jnp.bfloat16)
        band_power = local_power
        for shift in range(1, freq_size):
            band_power = band_power + lax.ppermute(sent_power, "freq", from_freq(shift)).astype(jnp.float32)
        factor = lax.rsqrt(band_power / total_bins + 1e-05) * valid.astype(jnp.float32)
        whitened = (spectrum_f32 * jnp.concatenate([factor, factor], axis=1)).astype(jnp.bfloat16)
        left = jnp.concatenate(
            [whitened, jnp.concatenate([whitened[:, window_count:], -whitened[:, :window_count]], axis=1)], axis=0
        )

        local_rel = station_index - group_index * chan_count
        selector = (local_rel[:, None] == jnp.arange(chan_count, dtype=jnp.int32)[None, :]).astype(jnp.bfloat16)
        stations = jnp.dot(selector, whitened, preferred_element_type=jnp.float32).astype(jnp.bfloat16)
        bit = 1
        while bit < group_size:
            stations = stations + lax.ppermute(stations, "grp", swap_by(bit))
            bit *= 2
        station_left = jnp.concatenate(
            [stations, jnp.concatenate([stations[:, window_count:], -stations[:, :window_count]], axis=1)], axis=0
        )
        kernel = lax.dot_general(station_left, whitened, ROWS_T, preferred_element_type=jnp.float32) * scaling
        station_count = station_index.shape[0]
        lags_here = LAGS // freq_size
        lag_values = (freq_index * lags_here + jnp.arange(lags_here, dtype=jnp.int32)).astype(jnp.float32)
        kernels, tables = [], []
        for shift in range(freq_size):
            got = kernel if shift == 0 else lax.ppermute(kernel, "freq", from_freq(shift))
            kernels.append(got.reshape(2, station_count, chan_count))
            bin_value = lax.rem(freq_index - shift + freq_size, freq_size).astype(jnp.float32) + 1.0
            phase = math.pi * bin_value * lag_values / LAGS
            tables.append(jnp.stack([jnp.cos(phase), -jnp.sin(phase)]))
        station_gather = jnp.einsum(
            "rsc,rl->scl",
            jnp.concatenate(kernels, axis=0),
            jnp.concatenate(tables, axis=0),
            precision=lax.Precision.HIGHEST,
        ) / math.sqrt(total_bins)

        half = chips // 2
        z, x = group_index // 4, lax.rem(group_index // 2, 2)
        place = jnp.where(x == 0, z, chips - 1 - z)
        sibling = lax.ppermute(whitened, "grp", swap_by(1))
        where = jnp.stack([group_index, group_index + 1 - 2 * core])
        cross = cross_blocks(left, whitened, sibling, where, None, total_chans, scaling)
        held = [whitened, sibling]
        step_sign = 1 - 2 * core
        for step in range(chips - 1):
            hop = step // 2 + 1
            got = lax.ppermute(held[step % 2], "grp", ring)
            held[step % 2] = got
            swapped = lax.ppermute(got, "grp", swap_by(1))
            kind = step % 2
            mine = block_of(place - hop * step_sign, core if kind == 0 else 1 - core, chips)
            other = block_of(place + hop * step_sign, 1 - core if kind == 0 else core, chips)
            cross = cross_blocks(left, got, swapped, jnp.stack([mine, other]), cross, total_chans, scaling)
        return (cross[None], station_gather)

    return on_device


def solution(mesh):
    placed = (P("freq", "grp", None), P("grp", None), P())
    return jax.shard_map(
        make_on_device(mesh.shape["grp"], mesh.shape["freq"]),
        mesh=mesh,
        in_specs=placed,
        out_specs=(P("freq", None, "grp", None), P(None, "grp", "freq")),
        check_vma=False,
    )
```

```python
import functools
import math

import jax
import jax.numpy as jnp
from jax import lax
from jax.experimental import pallas as pl
from jax.experimental.pallas import tpu as pltpu
from jax.sharding import PartitionSpec as P

LAGS = 256
ROWS_T = (((1,), (1,)), ((), ()))


def device_of(place, core, chips):
    place %= chips
    z, x = (place, 0) if place < chips // 2 else (chips - 1 - place, 1)
    return z * 4 + x * 2 + core


def place_of(device, chips):
    z, x = device // 4, device // 2 % 2
    return z if x == 0 else chips - 1 - z


def ring_pairs(group_size):
    chips = group_size // 2
    return [
        (device, device_of(place_of(device, chips) + 1 - 2 * (device % 2), device % 2, chips)) for device in range(group_size)
    ]


def block_of(place, core, chips):
    place = lax.rem(place + chips, chips)
    half = chips // 2
    return jnp.where(place < half, place * 4, (chips - 1 - place) * 4 + 2) + core


def own_block():
    return [lax.axis_index("grp")]


def sibling_block():
    group_index = lax.axis_index("grp")
    return [group_index + 1 - 2 * lax.rem(group_index, 2)]


def ring_blocks(step, chips):
    group_index = lax.axis_index("grp")
    core = lax.rem(group_index, 2)
    z, x = group_index // 4, lax.rem(group_index // 2, 2)
    place = jnp.where(x == 0, z, chips - 1 - z)
    back = (step // 2 + 1) * (1 - 2 * core)
    kept = core if step % 2 == 0 else 1 - core
    return [block_of(place - back, kept, chips), block_of(place + back, 1 - kept, chips)]


def cost(microseconds):
    return pl.CostEstimate(flops=int(microseconds * 1.15e9), bytes_accessed=0, transcendentals=0)


def split(values):
    terms = []
    for _ in range(3):
        term = lax.reduce_precision(values, 8, 7)
        terms.append(term.astype(jnp.bfloat16))
        values = values - term
    return terms


def band_powers(raw, chunks):
    rows, width = raw.shape[0], raw.shape[1] // 2

    def body(raw_ref, raw_out, *power_outs):
        for k, power_out in enumerate(power_outs):
            part = raw_ref[k * rows // chunks : (k + 1) * rows // chunks, :].astype(jnp.float32)
            power_out[...] = (part[:, :width] * part[:, :width] + part[:, width:] * part[:, width:]).astype(jnp.bfloat16)
        raw_out[...] = raw_ref[...]

    vmem = pl.BlockSpec(memory_space=pltpu.VMEM)
    return pl.pallas_call(
        body,
        out_shape=[jax.ShapeDtypeStruct(raw.shape, jnp.bfloat16)]
        + [jax.ShapeDtypeStruct((rows // chunks, width), jnp.bfloat16)] * chunks,
        in_specs=[vmem],
        out_specs=[vmem] * (1 + chunks),
        compiler_params=pltpu.CompilerParams(vmem_limit_bytes=8 * 2**20),
        cost_estimate=cost(0.1),
    )(raw)


def prepare(valid, station_index, after):
    rows, width = valid.shape
    stations = station_index.shape[0]

    def body(index_ref, valid_ref, _, valid_out, numbers_out, valid_held, index_held, sems):
        copies = [
            pltpu.make_async_copy(valid_ref, valid_held, sems.at[0]),
            pltpu.make_async_copy(index_ref, index_held, sems.at[1]),
        ]
        for copy in copies:
            copy.start()
        copies[1].wait()
        place = lax.broadcasted_iota(jnp.int32, (stations, rows), 0)
        numbers = jnp.zeros((stations, rows), jnp.int32)
        for k in range(stations):
            numbers = jnp.where(place == k, index_held[k], numbers)
        numbers_out[...] = numbers
        copies[0].wait()
        valid_out[...] = valid_held[...].astype(jnp.bfloat16)

    vmem, anywhere = pl.BlockSpec(memory_space=pltpu.VMEM), pl.BlockSpec(memory_space=pl.ANY)
    return pl.pallas_call(
        body,
        out_shape=[jax.ShapeDtypeStruct(valid.shape, jnp.bfloat16), jax.ShapeDtypeStruct((stations, rows), jnp.int32)],
        in_specs=[anywhere] * 3,
        out_specs=[vmem] * 2,
        scratch_shapes=[
            pltpu.VMEM(valid.shape, jnp.int32),
            pltpu.SMEM(station_index.shape, jnp.int32),
            pltpu.SemaphoreType.DMA((2,)),
        ],
        compiler_params=pltpu.CompilerParams(vmem_limit_bytes=8 * 2**20),
        cost_estimate=cost(0.3),
    )(station_index, valid, after)


def whiten(raw, valid, received, chunk, chunks, total_bins):
    rows, width = raw.shape[0] // chunks, raw.shape[1] // 2

    def body(raw_ref, valid_ref, *refs):
        part = raw_ref[...].astype(jnp.float32)
        real, imag = part[:, :width], part[:, width:]
        power = real * real + imag * imag
        for ref in refs[:-1]:
            power = power + ref[...].astype(jnp.float32)
        factor = lax.rsqrt(power / total_bins + 1e-05) * valid_ref[...].astype(jnp.float32)
        refs[-1][:, :width] = (real * factor).astype(jnp.bfloat16)
        refs[-1][:, width:] = (imag * factor).astype(jnp.bfloat16)

    vmem = pl.BlockSpec(memory_space=pltpu.VMEM)
    return pl.pallas_call(
        body,
        grid=(1,),
        out_shape=jax.ShapeDtypeStruct((rows, 2 * width), jnp.bfloat16),
        in_specs=[pl.BlockSpec((rows, 2 * width), lambda i: (chunk, 0)), pl.BlockSpec((rows, width), lambda i: (chunk, 0))]
        + [vmem] * len(received),
        out_specs=pl.BlockSpec((rows, 2 * width), lambda i: (0, 0)),
        compiler_params=pltpu.CompilerParams(vmem_limit_bytes=8 * 2**20),
        cost_estimate=cost(0.15),
    )(raw, valid, *received)


def cross_blocks(left, blocks, places, cross, total, scaling, numbers=None, stations=None, microseconds=0.0):
    rows, depth = blocks[0].shape
    count = len(blocks)
    vmem, anywhere = pl.BlockSpec(memory_space=pltpu.VMEM), pl.BlockSpec(memory_space=pl.ANY)
    operands = [left, *blocks]
    specs = [vmem] * len(operands)
    for more in (numbers, stations):
        if more is not None:
            operands.append(more)
            specs.append(vmem)
    aliases = {}
    if cross is not None:
        aliases = {len(operands): 0}
        operands.append(cross)
        specs.append(anywhere)
    shapes, out_specs = [jax.ShapeDtypeStruct((2, rows, total), jnp.bfloat16)], [anywhere]
    if numbers is not None:
        shapes.append(jax.ShapeDtypeStruct((numbers.shape[0], depth), jnp.bfloat16))
        out_specs.append(vmem)

    def body(left_ref, *refs):
        held, sems = refs[-2:]
        out_ref = refs[len(operands) - 1]
        copies, picked = [], None
        for k, place in enumerate(places()):
            product = lax.dot_general(left_ref[...], refs[k][...], ROWS_T, preferred_element_type=jnp.float32)
            held[k] = (product * scaling).astype(jnp.bfloat16).reshape(2, rows, rows)
            start = pl.multiple_of(place * rows, rows)
            copies.append(pltpu.make_async_copy(held.at[k], out_ref.at[:, :, pl.ds(start, rows)], sems.at[k]))
            copies[k].start()
            if numbers is not None:
                wanted = refs[count][...] - start
                selector = (wanted == lax.broadcasted_iota(jnp.int32, wanted.shape, 1)).astype(jnp.bfloat16)
                found = jnp.dot(selector, refs[k][...], preferred_element_type=jnp.float32)
                picked = found if picked is None else picked + found
        if numbers is not None:
            if stations is not None:
                picked = picked + refs[count + 1][...].astype(jnp.float32)
            refs[len(operands)][...] = picked.astype(jnp.bfloat16)
        for copy in copies:
            copy.wait()

    out = pl.pallas_call(
        body,
        out_shape=shapes,
        in_specs=specs,
        out_specs=out_specs,
        scratch_shapes=[pltpu.VMEM((count, 2, rows, rows), jnp.bfloat16), pltpu.SemaphoreType.DMA((count,))],
        input_output_aliases=aliases,
        compiler_params=pltpu.CompilerParams(vmem_limit_bytes=8 * 2**20),
        cost_estimate=cost(microseconds),
    )(*operands)
    return out if numbers is not None else out[0]


def make_on_device(group_size, freq_size):
    chips = group_size // 2
    ring = ring_pairs(group_size)

    def swap_by(bit):
        return [(g, g ^ bit) for g in range(group_size)]

    def swap(block, pieces=2):
        rows = block.shape[0] // pieces
        got = [lax.ppermute(block[k * rows : (k + 1) * rows], "grp", swap_by(1)) for k in range(pieces)]
        return got[0] if pieces == 1 else jnp.concatenate(got, axis=0)

    def from_freq(shift):
        return [(f, (f + shift) % freq_size) for f in range(freq_size)]

    def on_device(spectra, valid, station_index):
        bin_count, chan_count, double_width = spectra.shape
        assert bin_count == 1
        window_count = double_width // 2
        freq_index = lax.axis_index("freq")
        total_chans = chan_count * group_size
        total_bins = bin_count * freq_size
        scaling = 1.0 / math.sqrt(window_count)

        def to_kernel(stations, whitened):
            station_left = jnp.concatenate(
                [stations, jnp.concatenate([stations[:, window_count:], -stations[:, :window_count]], axis=1)], axis=0
            )
            kernel = lax.dot_general(station_left, whitened, ROWS_T, preferred_element_type=jnp.float32) * scaling
            kernels = [kernel]
            for shift in range(1, freq_size):
                kernels.append(lax.ppermute(kernel, "freq", from_freq(shift)))
            return kernels

        def to_lags(kernels):
            lags_here = LAGS // freq_size
            lag_values = (freq_index * lags_here + jnp.arange(lags_here, dtype=jnp.int32)).astype(jnp.float32)
            tables = []
            for shift in range(freq_size):
                bin_value = lax.rem(freq_index - shift + freq_size, freq_size).astype(jnp.float32) + 1.0
                phase = math.pi * bin_value * lag_values / LAGS
                tables += [jnp.cos(phase), -jnp.sin(phase)]
            table = jnp.stack(tables) / math.sqrt(total_bins)
            kernels = jnp.concatenate(kernels, axis=0).reshape(2 * freq_size, station_index.shape[0], chan_count)
            parts, table_parts = split(kernels), split(table)
            pairs = [(0, 0), (0, 1), (1, 0), (0, 2), (1, 1), (2, 0)]
            return jnp.einsum(
                "rsc,rl->scl",
                jnp.concatenate([parts[i] for i, _ in pairs], axis=0),
                jnp.concatenate([table_parts[j] for _, j in pairs], axis=0),
                preferred_element_type=jnp.float32,
            )

        chunks = 2
        raw, *powers = band_powers(spectra[0], chunks)
        valid, numbers = prepare(valid, station_index, raw)
        received = [[lax.ppermute(power, "freq", from_freq(shift)) for shift in range(1, freq_size)] for power in powers]

        parts = [whiten(raw, valid, received[0], 0, chunks, total_bins)]
        flying_parts = [lax.ppermute(parts[0], "grp", ring)]
        second, _ = lax.optimization_barrier((received[1], parts[0]))
        parts.append(whiten(raw, valid, second, 1, chunks, total_bins))
        flying_parts.append(lax.ppermute(parts[1], "grp", ring))
        whitened = jnp.concatenate(parts, axis=0)
        swapped = swap(whitened)
        flying = [None, lax.ppermute(swapped, "grp", ring)]
        left = jnp.concatenate(
            [whitened, jnp.concatenate([whitened[:, window_count:], -whitened[:, :window_count]], axis=1)], axis=0
        )
        later, flying_parts = lax.optimization_barrier((whitened, flying_parts))
        flying[0] = jnp.concatenate(flying_parts, axis=0)
        cross, stations = cross_blocks(left, [later], own_block, None, total_chans, scaling, numbers, None, 4.0)

        steps = chips - 1
        waiting, places = [], sibling_block
        for step in range(steps):
            arrived, cross, stations, swapped = lax.optimization_barrier((flying[step], cross, stations, swapped))
            if step + 2 < steps:
                flying.append(lax.ppermute(arrived, "grp", ring))
            next_swapped = swap(arrived)
            if step + 1 < steps:
                cross, stations = cross_blocks(left, [*waiting, swapped], places, cross, total_chans, scaling, numbers, stations)
            waiting, swapped, places = [arrived], next_swapped, functools.partial(ring_blocks, step, chips)
            if step + 2 == steps:
                cross, stations = cross_blocks(left, [*waiting, swapped], places, cross, total_chans, scaling, numbers, stations)
        cross, stations = cross_blocks(left, waiting, lambda: places()[:1], cross, total_chans, scaling, numbers, stations)
        cross, stations = cross_blocks(left, [swapped], lambda: places()[1:], cross, total_chans, scaling, numbers, stations)
        station_gather = to_lags(to_kernel(stations, whitened))
        return (cross[None], station_gather)

    return on_device


def solution(mesh):
    placed = (P("freq", "grp", None), P("grp", None), P())
    return jax.shard_map(
        make_on_device(mesh.shape["grp"], mesh.shape["freq"]),
        mesh=mesh,
        in_specs=placed,
        out_specs=(P("freq", None, "grp", None), P(None, "grp", "freq")),
        check_vma=False,
    )
```

```python
import functools
import math

import jax
import jax.numpy as jnp
from jax import lax
from jax.experimental import pallas as pl
from jax.experimental.pallas import tpu as pltpu
from jax.sharding import PartitionSpec as P

LAGS = 256
ROWS_T = (((1,), (1,)), ((), ()))


def device_of(place, core, chips):
    place %= chips
    z, x = (place, 0) if place < chips // 2 else (chips - 1 - place, 1)
    return z * 4 + x * 2 + core


def place_of(device, chips):
    z, x = device // 4, device // 2 % 2
    return z if x == 0 else chips - 1 - z


def ring_pairs(group_size):
    chips = group_size // 2
    return [
        (device, device_of(place_of(device, chips) + 1 - 2 * (device % 2), device % 2, chips)) for device in range(group_size)
    ]


def block_of(place, core, chips):
    place = lax.rem(place + chips, chips)
    half = chips // 2
    return jnp.where(place < half, place * 4, (chips - 1 - place) * 4 + 2) + core


def own_blocks():
    group_index = lax.axis_index("grp")
    return [group_index, group_index + 1 - 2 * lax.rem(group_index, 2)]


def ring_blocks(step, chips):
    group_index = lax.axis_index("grp")
    core = lax.rem(group_index, 2)
    z, x = group_index // 4, lax.rem(group_index // 2, 2)
    place = jnp.where(x == 0, z, chips - 1 - z)
    back = (step // 2 + 1) * (1 - 2 * core)
    kept = core if step % 2 == 0 else 1 - core
    return [block_of(place - back, kept, chips), block_of(place + back, 1 - kept, chips)]


def cost(microseconds):
    return pl.CostEstimate(flops=int(microseconds * 1.15e9), bytes_accessed=0, transcendentals=0)


def split(values):
    terms = []
    for _ in range(3):
        term = lax.reduce_precision(values, 8, 7)
        terms.append(term.astype(jnp.bfloat16))
        values = values - term
    return terms


def band_powers(raw, chunks):
    rows, width = raw.shape[0], raw.shape[1] // 2

    def body(raw_ref, raw_out, *power_outs):
        for k, power_out in enumerate(power_outs):
            part = raw_ref[k * rows // chunks : (k + 1) * rows // chunks, :].astype(jnp.float32)
            power_out[...] = (part[:, :width] * part[:, :width] + part[:, width:] * part[:, width:]).astype(jnp.bfloat16)
        raw_out[...] = raw_ref[...]

    vmem = pl.BlockSpec(memory_space=pltpu.VMEM)
    return pl.pallas_call(
        body,
        out_shape=[jax.ShapeDtypeStruct(raw.shape, jnp.bfloat16)]
        + [jax.ShapeDtypeStruct((rows // chunks, width), jnp.bfloat16)] * chunks,
        in_specs=[vmem],
        out_specs=[vmem] * (1 + chunks),
        compiler_params=pltpu.CompilerParams(vmem_limit_bytes=6 * 2**20),
        cost_estimate=cost(0.1),
    )(raw)


def prepare(valid, station_index, after):
    rows, width = valid.shape
    stations = station_index.shape[0]

    def body(index_ref, valid_ref, _, valid_out, numbers_out, valid_held, index_held, sems):
        copies = [
            pltpu.make_async_copy(valid_ref, valid_held, sems.at[0]),
            pltpu.make_async_copy(index_ref, index_held, sems.at[1]),
        ]
        for copy in copies:
            copy.start()
        copies[1].wait()
        place = lax.broadcasted_iota(jnp.int32, (stations, rows), 0)
        numbers = jnp.zeros((stations, rows), jnp.int32)
        for k in range(stations):
            numbers = jnp.where(place == k, index_held[k], numbers)
        numbers_out[...] = numbers
        copies[0].wait()
        valid_out[...] = valid_held[...].astype(jnp.bfloat16)

    vmem, anywhere = pl.BlockSpec(memory_space=pltpu.VMEM), pl.BlockSpec(memory_space=pl.ANY)
    return pl.pallas_call(
        body,
        out_shape=[jax.ShapeDtypeStruct(valid.shape, jnp.bfloat16), jax.ShapeDtypeStruct((stations, rows), jnp.int32)],
        in_specs=[anywhere] * 3,
        out_specs=[vmem] * 2,
        scratch_shapes=[
            pltpu.VMEM(valid.shape, jnp.int32),
            pltpu.SMEM(station_index.shape, jnp.int32),
            pltpu.SemaphoreType.DMA((2,)),
        ],
        compiler_params=pltpu.CompilerParams(vmem_limit_bytes=6 * 2**20),
        cost_estimate=cost(0.3),
    )(station_index, valid, after)


def whiten(raw, valid, received, chunk, chunks, total_bins):
    rows, width = raw.shape[0] // chunks, raw.shape[1] // 2

    def body(raw_ref, valid_ref, *refs):
        part = raw_ref[...].astype(jnp.float32)
        real, imag = part[:, :width], part[:, width:]
        power = real * real + imag * imag
        for ref in refs[:-1]:
            power = power + ref[...].astype(jnp.float32)
        factor = lax.rsqrt(power / total_bins + 1e-05) * valid_ref[...].astype(jnp.float32)
        refs[-1][:, :width] = (real * factor).astype(jnp.bfloat16)
        refs[-1][:, width:] = (imag * factor).astype(jnp.bfloat16)

    vmem = pl.BlockSpec(memory_space=pltpu.VMEM)
    return pl.pallas_call(
        body,
        grid=(1,),
        out_shape=jax.ShapeDtypeStruct((rows, 2 * width), jnp.bfloat16),
        in_specs=[pl.BlockSpec((rows, 2 * width), lambda i: (chunk, 0)), pl.BlockSpec((rows, width), lambda i: (chunk, 0))]
        + [vmem] * len(received),
        out_specs=pl.BlockSpec((rows, 2 * width), lambda i: (0, 0)),
        compiler_params=pltpu.CompilerParams(vmem_limit_bytes=6 * 2**20),
        cost_estimate=cost(0.7),
    )(raw, valid, *received)


def select(numbers, first):
    wanted = numbers - first
    return (wanted == lax.broadcasted_iota(jnp.int32, wanted.shape, 1)).astype(jnp.bfloat16)


def pick(block, numbers, places):
    def body(block_ref, numbers_ref, out_ref):
        selector = select(numbers_ref[...], places()[0] * block_ref.shape[0])
        out_ref[...] = jnp.dot(selector, block_ref[...], preferred_element_type=jnp.float32).astype(jnp.bfloat16)

    vmem = pl.BlockSpec(memory_space=pltpu.VMEM)
    return pl.pallas_call(
        body,
        out_shape=jax.ShapeDtypeStruct((numbers.shape[0], block.shape[1]), jnp.bfloat16),
        in_specs=[vmem, vmem],
        out_specs=vmem,
        compiler_params=pltpu.CompilerParams(vmem_limit_bytes=6 * 2**20),
        cost_estimate=cost(0.1),
    )(block, numbers)


def cross_blocks(left, blocks, places, cross, total, scaling, numbers=None, stations=None, microseconds=0.0):
    rows, depth = left.shape[0] // 2, left.shape[1]
    pieces = [len(block) for block in blocks]
    count = sum(pieces)
    vmem, anywhere = pl.BlockSpec(memory_space=pltpu.VMEM), pl.BlockSpec(memory_space=pl.ANY)
    operands = [left, *(piece for block in blocks for piece in block)]
    specs = [vmem] * len(operands)
    for more in (numbers, stations):
        if more is not None:
            operands.append(more)
            specs.append(vmem)
    aliases = {}
    if cross is not None:
        aliases = {len(operands): 0}
        operands.append(cross)
        specs.append(anywhere)
    shapes, out_specs = [jax.ShapeDtypeStruct((2, rows, total), jnp.bfloat16)], [anywhere]
    if numbers is not None:
        shapes.append(jax.ShapeDtypeStruct((numbers.shape[0], depth), jnp.bfloat16))
        out_specs.append(vmem)

    def body(left_ref, *refs):
        held, sems = refs[-2:]
        out_ref = refs[len(operands) - 1]
        copies, picked = [], None
        for k, place in enumerate(places()):
            first = sum(pieces[:k])
            block = jnp.concatenate([ref[...] for ref in refs[first : first + pieces[k]]], axis=0)
            product = lax.dot_general(left_ref[...], block, ROWS_T, preferred_element_type=jnp.float32)
            held[k] = (product * scaling).astype(jnp.bfloat16).reshape(2, rows, rows)
            start = pl.multiple_of(place * rows, rows)
            copies.append(pltpu.make_async_copy(held.at[k], out_ref.at[:, :, pl.ds(start, rows)], sems.at[k]))
            copies[k].start()
            if numbers is not None:
                found = jnp.dot(select(refs[count][...], start), block, preferred_element_type=jnp.float32)
                picked = found if picked is None else picked + found
        if numbers is not None:
            if stations is not None:
                picked = picked + refs[count + 1][...].astype(jnp.float32)
            refs[len(operands)][...] = picked.astype(jnp.bfloat16)
        for copy in copies:
            copy.wait()

    out = pl.pallas_call(
        body,
        out_shape=shapes,
        in_specs=specs,
        out_specs=out_specs,
        scratch_shapes=[
            pltpu.VMEM((len(blocks), 2, rows, rows), jnp.bfloat16),
            pltpu.SemaphoreType.DMA((len(blocks),)),
        ],
        input_output_aliases=aliases,
        compiler_params=pltpu.CompilerParams(vmem_limit_bytes=6 * 2**20),
        cost_estimate=cost(microseconds),
    )(*operands)
    return out if numbers is not None else out[0]


def station_kernel(parts, left, scaling):
    rows, width = left.shape[0] // 2, left.shape[1] // 2
    stations = parts[0].shape[0]

    def body(left_ref, *refs):
        found = sum(ref[...].astype(jnp.float32) for ref in refs[:-1])
        turned = jnp.concatenate([found[:, width:], -found[:, :width]], axis=1)
        both = jnp.concatenate([found, turned], axis=0).astype(jnp.bfloat16)
        refs[-1][...] = lax.dot_general(both, left_ref[:rows, :], ROWS_T, preferred_element_type=jnp.float32) * scaling

    vmem = pl.BlockSpec(memory_space=pltpu.VMEM)
    return pl.pallas_call(
        body,
        out_shape=jax.ShapeDtypeStruct((2 * stations, rows), jnp.float32),
        in_specs=[vmem] * (1 + len(parts)),
        out_specs=vmem,
        compiler_params=pltpu.CompilerParams(vmem_limit_bytes=6 * 2**20),
        cost_estimate=cost(0.2),
    )(left, *parts)


def make_on_device(group_size, freq_size):
    chips = group_size // 2
    ring = ring_pairs(group_size)

    def swap_by(bit):
        return [(g, g ^ bit) for g in range(group_size)]

    def swap_pieces(block, pieces):
        rows = block.shape[0] // pieces
        return [lax.ppermute(block[k * rows : (k + 1) * rows], "grp", swap_by(1)) for k in range(pieces)]

    def swap(block):
        return swap_pieces(block, 2)

    def from_freq(shift):
        return [(f, (f + shift) % freq_size) for f in range(freq_size)]

    def on_device(spectra, valid, station_index):
        bin_count, chan_count, double_width = spectra.shape
        assert bin_count == 1
        window_count = double_width // 2
        freq_index = lax.axis_index("freq")
        total_chans = chan_count * group_size
        total_bins = bin_count * freq_size
        scaling = 1.0 / math.sqrt(window_count)

        def to_kernel(stations):
            kernel = station_kernel(stations, left, scaling)
            return [kernel] + [lax.ppermute(kernel, "freq", from_freq(shift)) for shift in range(1, freq_size)]

        def to_lags(kernels):
            lags_here = LAGS // freq_size
            lag_values = (freq_index * lags_here + jnp.arange(lags_here, dtype=jnp.int32)).astype(jnp.float32)
            tables = []
            for shift in range(freq_size):
                bin_value = lax.rem(freq_index - shift + freq_size, freq_size).astype(jnp.float32) + 1.0
                phase = math.pi * bin_value * lag_values / LAGS
                tables += [jnp.cos(phase), -jnp.sin(phase)]
            table = jnp.stack(tables) / math.sqrt(total_bins)
            kernels = jnp.concatenate(kernels, axis=0).reshape(2 * freq_size, station_index.shape[0], chan_count)
            parts, table_parts = split(kernels), split(table)
            pairs = [(0, 0), (0, 1), (1, 0), (0, 2), (1, 1), (2, 0)]
            return jnp.einsum(
                "rsc,rl->scl",
                jnp.concatenate([parts[i] for i, _ in pairs], axis=0),
                jnp.concatenate([table_parts[j] for _, j in pairs], axis=0),
                preferred_element_type=jnp.float32,
            )

        chunks = 2
        raw, *powers = band_powers(spectra[0], chunks)
        valid, numbers = prepare(valid, station_index, raw)
        received = [[lax.ppermute(power, "freq", from_freq(shift)) for shift in range(1, freq_size)] for power in powers]

        parts = [whiten(raw, valid, received[0], 0, chunks, total_bins)]
        flying_parts = [lax.ppermute(parts[0], "grp", ring)]
        swapped = swap_pieces(parts[0], 2)
        second, _ = lax.optimization_barrier((received[1], parts[0]))
        parts.append(whiten(raw, valid, second, 1, chunks, total_bins))
        second, swapped[0] = lax.optimization_barrier((parts[1], swapped[0]))
        flying_parts.append(lax.ppermute(second, "grp", ring))
        swapped += swap_pieces(parts[1], 2)
        whitened = jnp.concatenate(parts, axis=0)
        flying = [None, lax.ppermute(jnp.concatenate(swapped, axis=0), "grp", ring)]
        left = jnp.concatenate(
            [whitened, jnp.concatenate([whitened[:, window_count:], -whitened[:, :window_count]], axis=1)], axis=0
        )
        later, flying_parts[0] = lax.optimization_barrier((whitened, flying_parts[0]))
        cross, stations = cross_blocks(
            left, [[later], swapped], own_blocks, None, total_chans, scaling, numbers, None, 4.0
        )
        flying[0] = jnp.concatenate(flying_parts, axis=0)

        steps = chips - 1
        waiting = []
        for step in range(steps):
            arrived, cross, stations, swapped = lax.optimization_barrier((flying[step], cross, stations, swapped))
            if step + 2 < steps:
                flying.append(lax.ppermute(arrived, "grp", ring))
            next_swapped = swap(arrived)
            if waiting and step + 1 < steps:
                cross, stations = cross_blocks(left, [waiting, swapped], places, cross, total_chans, scaling, numbers, stations)
            waiting, swapped, places = [arrived], next_swapped, functools.partial(ring_blocks, step, chips)
            if step + 2 == steps:
                cross, stations = cross_blocks(left, [waiting, swapped], places, cross, total_chans, scaling, numbers, stations)
        found = pick(waiting[0], numbers, places)
        kernels = to_kernel([stations, found, lax.ppermute(found, "grp", swap_by(1))])
        cross = cross_blocks(left, [waiting, swapped], places, cross, total_chans, scaling)
        kernels, cross = lax.optimization_barrier((kernels, cross))
        station_gather = to_lags(kernels)
        return (cross[None], station_gather)

    return on_device


def solution(mesh):
    placed = (P("freq", "grp", None), P("grp", None), P())
    return jax.shard_map(
        make_on_device(mesh.shape["grp"], mesh.shape["freq"]),
        mesh=mesh,
        in_specs=placed,
        out_specs=(P("freq", None, "grp", None), P(None, "grp", "freq")),
        check_vma=False,
    )
```

```python
import functools
import math

import jax
import jax.numpy as jnp
from jax import lax
from jax.experimental import pallas as pl
from jax.experimental.pallas import tpu as pltpu
from jax.sharding import PartitionSpec as P

LAGS = 256
ROWS_T = (((1,), (1,)), ((), ()))


def device_of(place, core, chips):
    place %= chips
    z, x = (place, 0) if place < chips // 2 else (chips - 1 - place, 1)
    return z * 4 + x * 2 + core


def place_of(device, chips):
    z, x = device // 4, device // 2 % 2
    return z if x == 0 else chips - 1 - z


def ring_pairs(group_size):
    chips = group_size // 2
    return [
        (device, device_of(place_of(device, chips) + 1 - 2 * (device % 2), device % 2, chips)) for device in range(group_size)
    ]


def block_of(place, core, chips):
    place = lax.rem(place + chips, chips)
    half = chips // 2
    return jnp.where(place < half, place * 4, (chips - 1 - place) * 4 + 2) + core


def own_blocks():
    group_index = lax.axis_index("grp")
    return [group_index, group_index + 1 - 2 * lax.rem(group_index, 2)]


def ring_blocks(step, chips):
    group_index = lax.axis_index("grp")
    core = lax.rem(group_index, 2)
    z, x = group_index // 4, lax.rem(group_index // 2, 2)
    place = jnp.where(x == 0, z, chips - 1 - z)
    back = (step // 2 + 1) * (1 - 2 * core)
    kept = core if step % 2 == 0 else 1 - core
    return [block_of(place - back, kept, chips), block_of(place + back, 1 - kept, chips)]


def cost(microseconds):
    return pl.CostEstimate(flops=int(microseconds * 1.15e9), bytes_accessed=0, transcendentals=0)


def band_powers(raw, chunks):
    rows, width = raw.shape[0], raw.shape[1] // 2

    def body(raw_ref, raw_out, *power_outs):
        for k, power_out in enumerate(power_outs):
            part = raw_ref[k * rows // chunks : (k + 1) * rows // chunks, :].astype(jnp.float32)
            power_out[...] = (part[:, :width] * part[:, :width] + part[:, width:] * part[:, width:]).astype(jnp.bfloat16)
        raw_out[...] = raw_ref[...]

    vmem = pl.BlockSpec(memory_space=pltpu.VMEM)
    return pl.pallas_call(
        body,
        out_shape=[jax.ShapeDtypeStruct(raw.shape, jnp.bfloat16)]
        + [jax.ShapeDtypeStruct((rows // chunks, width), jnp.bfloat16)] * chunks,
        in_specs=[vmem],
        out_specs=[vmem] * (1 + chunks),
        compiler_params=pltpu.CompilerParams(vmem_limit_bytes=6 * 2**20),
        cost_estimate=cost(0.1),
    )(raw)


def prepare(valid, station_index, after):
    rows, width = valid.shape
    stations = station_index.shape[0]

    def body(index_ref, valid_ref, _, valid_out, numbers_out, valid_held, index_held, sems):
        copies = [
            pltpu.make_async_copy(valid_ref, valid_held, sems.at[0]),
            pltpu.make_async_copy(index_ref, index_held, sems.at[1]),
        ]
        for copy in copies:
            copy.start()
        copies[1].wait()
        place = lax.broadcasted_iota(jnp.int32, (stations, rows), 0)
        numbers = jnp.zeros((stations, rows), jnp.int32)
        for k in range(stations):
            numbers = jnp.where(place == k, index_held[k], numbers)
        numbers_out[...] = numbers
        copies[0].wait()
        valid_out[...] = valid_held[...].astype(jnp.bfloat16)

    vmem, anywhere = pl.BlockSpec(memory_space=pltpu.VMEM), pl.BlockSpec(memory_space=pl.ANY)
    return pl.pallas_call(
        body,
        out_shape=[jax.ShapeDtypeStruct(valid.shape, jnp.bfloat16), jax.ShapeDtypeStruct((stations, rows), jnp.int32)],
        in_specs=[anywhere] * 3,
        out_specs=[vmem] * 2,
        scratch_shapes=[
            pltpu.VMEM(valid.shape, jnp.int32),
            pltpu.SMEM(station_index.shape, jnp.int32),
            pltpu.SemaphoreType.DMA((2,)),
        ],
        compiler_params=pltpu.CompilerParams(vmem_limit_bytes=6 * 2**20),
        cost_estimate=cost(0.3),
    )(station_index, valid, after)


def whiten(raw, valid, received, chunk, chunks, total_bins):
    rows, width = raw.shape[0] // chunks, raw.shape[1] // 2

    def body(raw_ref, valid_ref, *refs):
        part = raw_ref[...].astype(jnp.float32)
        real, imag = part[:, :width], part[:, width:]
        power = real * real + imag * imag
        for ref in refs[:-1]:
            power = power + ref[...].astype(jnp.float32)
        factor = lax.rsqrt(power / total_bins + 1e-05) * valid_ref[...].astype(jnp.float32)
        refs[-1][:, :width] = (real * factor).astype(jnp.bfloat16)
        refs[-1][:, width:] = (imag * factor).astype(jnp.bfloat16)

    vmem = pl.BlockSpec(memory_space=pltpu.VMEM)
    return pl.pallas_call(
        body,
        grid=(1,),
        out_shape=jax.ShapeDtypeStruct((rows, 2 * width), jnp.bfloat16),
        in_specs=[pl.BlockSpec((rows, 2 * width), lambda i: (chunk, 0)), pl.BlockSpec((rows, width), lambda i: (chunk, 0))]
        + [vmem] * len(received),
        out_specs=pl.BlockSpec((rows, 2 * width), lambda i: (0, 0)),
        compiler_params=pltpu.CompilerParams(vmem_limit_bytes=6 * 2**20),
        cost_estimate=cost(0.7),
    )(raw, valid, *received)


def select(numbers, first):
    wanted = numbers - first
    return (wanted == lax.broadcasted_iota(jnp.int32, wanted.shape, 1)).astype(jnp.bfloat16)


def pick(block, numbers, places):
    def body(block_ref, numbers_ref, out_ref):
        selector = select(numbers_ref[...], places()[0] * block_ref.shape[0])
        out_ref[...] = jnp.dot(selector, block_ref[...], preferred_element_type=jnp.float32).astype(jnp.bfloat16)

    vmem = pl.BlockSpec(memory_space=pltpu.VMEM)
    return pl.pallas_call(
        body,
        out_shape=jax.ShapeDtypeStruct((numbers.shape[0], block.shape[1]), jnp.bfloat16),
        in_specs=[vmem, vmem],
        out_specs=vmem,
        compiler_params=pltpu.CompilerParams(vmem_limit_bytes=6 * 2**20),
        cost_estimate=cost(0.1),
    )(block, numbers)


def cross_blocks(left, blocks, places, cross, total, scaling, numbers=None, stations=None, microseconds=0.0):
    rows, depth = left.shape[0] // 2, left.shape[1]
    pieces = [len(block) for block in blocks]
    count = sum(pieces)
    vmem, anywhere = pl.BlockSpec(memory_space=pltpu.VMEM), pl.BlockSpec(memory_space=pl.ANY)
    operands = [left, *(piece for block in blocks for piece in block)]
    specs = [vmem] * len(operands)
    for more in (numbers, stations):
        if more is not None:
            operands.append(more)
            specs.append(vmem)
    aliases = {}
    if cross is not None:
        aliases = {len(operands): 0}
        operands.append(cross)
        specs.append(anywhere)
    shapes, out_specs = [jax.ShapeDtypeStruct((2, rows, total), jnp.bfloat16)], [anywhere]
    if numbers is not None:
        shapes.append(jax.ShapeDtypeStruct((numbers.shape[0], depth), jnp.bfloat16))
        out_specs.append(vmem)

    def body(left_ref, *refs):
        held, sems = refs[-2:]
        out_ref = refs[len(operands) - 1]
        copies, picked = [], None
        for k, place in enumerate(places()):
            first = sum(pieces[:k])
            block = jnp.concatenate([ref[...] for ref in refs[first : first + pieces[k]]], axis=0)
            product = lax.dot_general(left_ref[...], block, ROWS_T, preferred_element_type=jnp.float32)
            held[k] = (product * scaling).astype(jnp.bfloat16).reshape(2, rows, rows)
            start = pl.multiple_of(place * rows, rows)
            copies.append(pltpu.make_async_copy(held.at[k], out_ref.at[:, :, pl.ds(start, rows)], sems.at[k]))
            copies[k].start()
            if numbers is not None:
                found = jnp.dot(select(refs[count][...], start), block, preferred_element_type=jnp.float32)
                picked = found if picked is None else picked + found
        if numbers is not None:
            if stations is not None:
                picked = picked + refs[count + 1][...].astype(jnp.float32)
            refs[len(operands)][...] = picked.astype(jnp.bfloat16)
        for copy in copies:
            copy.wait()

    out = pl.pallas_call(
        body,
        out_shape=shapes,
        in_specs=specs,
        out_specs=out_specs,
        scratch_shapes=[
            pltpu.VMEM((len(blocks), 2, rows, rows), jnp.bfloat16),
            pltpu.SemaphoreType.DMA((len(blocks),)),
        ],
        input_output_aliases=aliases,
        compiler_params=pltpu.CompilerParams(vmem_limit_bytes=6 * 2**20),
        cost_estimate=cost(microseconds),
    )(*operands)
    return out if numbers is not None else out[0]


def station_kernel(parts, left, scaling):
    rows, width = left.shape[0] // 2, left.shape[1] // 2
    stations = parts[0].shape[0]

    def body(left_ref, *refs):
        found = sum(ref[...].astype(jnp.float32) for ref in refs[:-1])
        turned = jnp.concatenate([found[:, width:], -found[:, :width]], axis=1)
        both = jnp.concatenate([found, turned], axis=0).astype(jnp.bfloat16)
        refs[-1][...] = lax.dot_general(both, left_ref[:rows, :], ROWS_T, preferred_element_type=jnp.float32) * scaling

    vmem = pl.BlockSpec(memory_space=pltpu.VMEM)
    return pl.pallas_call(
        body,
        out_shape=jax.ShapeDtypeStruct((2 * stations, rows), jnp.float32),
        in_specs=[vmem] * (1 + len(parts)),
        out_specs=vmem,
        compiler_params=pltpu.CompilerParams(vmem_limit_bytes=6 * 2**20),
        cost_estimate=cost(0.2),
    )(left, *parts)


def spread(table, stations):
    parts, lags = table.shape
    high = lax.reduce_precision(table, 8, 7)
    low = table - high
    same = jnp.eye(stations, dtype=jnp.float32)[None, :, :, None]

    def blocks(values):
        return (values[:, None, None, :] * same).reshape(parts * stations, stations * lags).astype(jnp.bfloat16)

    return jnp.concatenate([blocks(high), blocks(low), blocks(high)], axis=0)


def lag_sums(kernels, table):
    rows = kernels[0].shape[1]
    stations = kernels[0].shape[0] // 2
    lags = table.shape[1] // stations
    groups = 4
    each = stations // groups

    def body(table_ref, *refs):
        out_ref, held, sems = refs[-3:]
        parts = jnp.concatenate([ref[...] for ref in refs[:-3]], axis=0)
        high = parts.astype(jnp.bfloat16).astype(jnp.float32)
        columns = jnp.concatenate([high, high, parts - high], axis=0).T.astype(jnp.bfloat16)
        copies = []
        for group in range(groups):
            part = slice(group * each * lags, (group + 1) * each * lags)
            sums = jnp.dot(columns, table_ref[:, part], preferred_element_type=jnp.float32)
            for k in range(each):
                held[group * each + k] = sums[:, k * lags : (k + 1) * lags]
            part = pl.ds(group * each, each)
            copies.append(pltpu.make_async_copy(held.at[part], out_ref.at[part], sems.at[group]))
            copies[group].start()
        for copy in copies:
            copy.wait()

    vmem = pl.BlockSpec(memory_space=pltpu.VMEM)
    return pl.pallas_call(
        body,
        out_shape=jax.ShapeDtypeStruct((stations, rows, lags), jnp.float32),
        in_specs=[vmem] * (1 + len(kernels)),
        out_specs=pl.BlockSpec(memory_space=pl.ANY),
        scratch_shapes=[pltpu.VMEM((stations, rows, lags), jnp.float32), pltpu.SemaphoreType.DMA((groups,))],
        compiler_params=pltpu.CompilerParams(vmem_limit_bytes=8 * 2**20),
        cost_estimate=cost(8.0),
    )(table, *kernels)


def make_on_device(group_size, freq_size):
    chips = group_size // 2
    ring = ring_pairs(group_size)
    across = [
        (device, device_of(place_of(device, chips) - 1 + 2 * (device % 2), 1 - device % 2, chips)) for device in range(group_size)
    ]

    def swap_by(bit):
        return [(g, g ^ bit) for g in range(group_size)]

    def swap_pieces(block, pieces):
        rows = block.shape[0] // pieces
        return [lax.ppermute(block[k * rows : (k + 1) * rows], "grp", swap_by(1)) for k in range(pieces)]

    def swap(block):
        return swap_pieces(block, 2)

    def from_freq(shift):
        return [(f, (f + shift) % freq_size) for f in range(freq_size)]

    def on_device(spectra, valid, station_index):
        bin_count, chan_count, double_width = spectra.shape
        assert bin_count == 1
        window_count = double_width // 2
        freq_index = lax.axis_index("freq")
        total_chans = chan_count * group_size
        total_bins = bin_count * freq_size
        scaling = 1.0 / math.sqrt(window_count)

        station_count = station_index.shape[0]
        lags_here = LAGS // freq_size
        lag_values = (freq_index * lags_here + jnp.arange(lags_here, dtype=jnp.int32)).astype(jnp.float32)
        tables = []
        for shift in range(freq_size):
            bin_value = lax.rem(freq_index - shift + freq_size, freq_size).astype(jnp.float32) + 1.0
            phase = math.pi * bin_value * lag_values / LAGS
            tables += [jnp.cos(phase), -jnp.sin(phase)]
        table = spread(jnp.stack(tables) / math.sqrt(total_bins), station_count)

        chunks = 2
        raw, *powers = band_powers(spectra[0], chunks)
        valid, numbers = prepare(valid, station_index, raw)
        received = [[lax.ppermute(power, "freq", from_freq(shift)) for shift in range(1, freq_size)] for power in powers]

        parts = [whiten(raw, valid, received[0], 0, chunks, total_bins)]
        flying_parts = [lax.ppermute(parts[0], "grp", ring)]
        swapped = swap_pieces(parts[0], 2)
        second, _ = lax.optimization_barrier((received[1], parts[0]))
        parts.append(whiten(raw, valid, second, 1, chunks, total_bins))
        second, swapped[0] = lax.optimization_barrier((parts[1], swapped[0]))
        flying_parts.append(lax.ppermute(second, "grp", ring))
        swapped += swap_pieces(parts[1], 2)
        whitened = jnp.concatenate(parts, axis=0)
        flying = [None, lax.ppermute(jnp.concatenate(swapped, axis=0), "grp", ring)]
        left = jnp.concatenate(
            [whitened, jnp.concatenate([whitened[:, window_count:], -whitened[:, :window_count]], axis=1)], axis=0
        )
        later, flying_parts[0] = lax.optimization_barrier((whitened, flying_parts[0]))
        cross, stations = cross_blocks(
            left, [[later], swapped], own_blocks, None, total_chans, scaling, numbers, None, 4.0
        )
        flying[0] = jnp.concatenate(flying_parts, axis=0)

        steps = chips - 1
        waiting, ahead, kernels = [], [], []
        for step in range(steps):
            arrived, cross, stations, swapped, ahead, kernels = lax.optimization_barrier(
                (flying[step], cross, stations, swapped, ahead, kernels)
            )
            if step + 2 < steps:
                flying.append(lax.ppermute(arrived, "grp", ring))
            if step + 3 == steps:
                found = pick(arrived, numbers, functools.partial(ring_blocks, step, chips))
                ahead = [lax.ppermute(lax.ppermute(found, "grp", swap_by(1)), "grp", across)]
            if step == 2:
                table, cross = lax.optimization_barrier((table, cross))
            if step + 2 == steps:
                ahead.append(lax.ppermute(ahead[0], "grp", swap_by(1)))
            next_swapped = swap(arrived)
            if waiting and step + 1 < steps:
                cross, stations = cross_blocks(left, [waiting, swapped], places, cross, total_chans, scaling, numbers, stations)
            waiting, swapped, places = [arrived], next_swapped, functools.partial(ring_blocks, step, chips)
            if step + 2 == steps:
                cross, stations = cross_blocks(left, [waiting, swapped], places, cross, total_chans, scaling, numbers, stations)
                kernels = [station_kernel([stations, *ahead], left, scaling)]
                others = [lax.ppermute(kernels[0], "freq", from_freq(shift)) for shift in range(1, freq_size)]
        station_gather = lag_sums(kernels + others, table)
        cross = cross_blocks(left, [waiting, swapped], places, cross, total_chans, scaling)
        return (cross[None], station_gather)

    return on_device


def solution(mesh):
    placed = (P("freq", "grp", None), P("grp", None), P())
    return jax.shard_map(
        make_on_device(mesh.shape["grp"], mesh.shape["freq"]),
        mesh=mesh,
        in_specs=placed,
        out_specs=(P("freq", None, "grp", None), P(None, "grp", "freq")),
        check_vma=False,
    )
```

```python
import functools
import math

import jax
import jax.numpy as jnp
from jax import lax
from jax.experimental import pallas as pl
from jax.experimental.pallas import tpu as pltpu
from jax.sharding import PartitionSpec as P

LAGS = 256
ROWS_T = (((1,), (1,)), ((), ()))


def device_of(place, core, chips):
    place %= chips
    z, x = (place, 0) if place < chips // 2 else (chips - 1 - place, 1)
    return z * 4 + x * 2 + core


def place_of(device, chips):
    z, x = device // 4, device // 2 % 2
    return z if x == 0 else chips - 1 - z


def ring_pairs(group_size):
    chips = group_size // 2
    return [
        (device, device_of(place_of(device, chips) + 1 - 2 * (device % 2), device % 2, chips)) for device in range(group_size)
    ]


def block_of(place, core, chips):
    place = lax.rem(place + chips, chips)
    half = chips // 2
    return jnp.where(place < half, place * 4, (chips - 1 - place) * 4 + 2) + core


def own_blocks():
    group_index = lax.axis_index("grp")
    return [group_index, group_index + 1 - 2 * lax.rem(group_index, 2)]


def ring_blocks(step, chips):
    group_index = lax.axis_index("grp")
    core = lax.rem(group_index, 2)
    z, x = group_index // 4, lax.rem(group_index // 2, 2)
    place = jnp.where(x == 0, z, chips - 1 - z)
    back = (step // 2 + 1) * (1 - 2 * core)
    kept = core if step % 2 == 0 else 1 - core
    return [block_of(place - back, kept, chips), block_of(place + back, 1 - kept, chips)]


def cost(microseconds):
    return pl.CostEstimate(flops=int(microseconds * 1.15e9), bytes_accessed=0, transcendentals=0)


def band_power(raw):
    rows, width = raw.shape[0], raw.shape[1] // 2

    def body(raw_ref, raw_out, power_out):
        part = raw_ref[...].astype(jnp.float32)
        power_out[...] = (part[:, :width] * part[:, :width] + part[:, width:] * part[:, width:]).astype(jnp.bfloat16)
        raw_out[...] = raw_ref[...]

    vmem = pl.BlockSpec(memory_space=pltpu.VMEM)
    return pl.pallas_call(
        body,
        out_shape=[jax.ShapeDtypeStruct(raw.shape, jnp.bfloat16), jax.ShapeDtypeStruct((rows, width), jnp.bfloat16)],
        in_specs=[vmem],
        out_specs=[vmem, vmem],
        compiler_params=pltpu.CompilerParams(vmem_limit_bytes=6 * 2**20),
        cost_estimate=cost(0.1),
    )(raw)


def prepare(valid, station_index, after):
    rows, width = valid.shape
    stations = station_index.shape[0]

    def body(index_ref, valid_ref, _, valid_out, numbers_out, valid_held, index_held, sems):
        copies = [
            pltpu.make_async_copy(valid_ref, valid_held, sems.at[0]),
            pltpu.make_async_copy(index_ref, index_held, sems.at[1]),
        ]
        for copy in copies:
            copy.start()
        copies[1].wait()
        place = lax.broadcasted_iota(jnp.int32, (stations, rows), 0)
        numbers = jnp.zeros((stations, rows), jnp.int32)
        for k in range(stations):
            numbers = jnp.where(place == k, index_held[k], numbers)
        numbers_out[...] = numbers
        copies[0].wait()
        valid_out[...] = valid_held[...].astype(jnp.bfloat16)

    vmem, anywhere = pl.BlockSpec(memory_space=pltpu.VMEM), pl.BlockSpec(memory_space=pl.ANY)
    return pl.pallas_call(
        body,
        out_shape=[jax.ShapeDtypeStruct(valid.shape, jnp.bfloat16), jax.ShapeDtypeStruct((stations, rows), jnp.int32)],
        in_specs=[anywhere] * 3,
        out_specs=[vmem] * 2,
        scratch_shapes=[
            pltpu.VMEM(valid.shape, jnp.int32),
            pltpu.SMEM(station_index.shape, jnp.int32),
            pltpu.SemaphoreType.DMA((2,)),
        ],
        compiler_params=pltpu.CompilerParams(vmem_limit_bytes=6 * 2**20),
        cost_estimate=cost(0.3),
    )(station_index, valid, after)


def whiten_rows(raw, others, total_bins):
    part = raw.astype(jnp.float32)
    width = part.shape[1] // 2
    real, imag = part[:, :width], part[:, width:]
    power = real * real + imag * imag + others
    factor = jnp.where(others < 0.0, 0.0, lax.rsqrt(power / total_bins + 1e-05))
    return (real * factor).astype(jnp.bfloat16), (imag * factor).astype(jnp.bfloat16)


def whiten_own(raw, valid, received, total_bins):
    rows, width = valid.shape

    def body(raw_ref, valid_ref, *refs):
        others = sum(ref[...].astype(jnp.float32) for ref in refs[:-2])
        others = jnp.where(valid_ref[...].astype(jnp.float32) > 0.0, others, -1.0).astype(jnp.bfloat16)
        refs[-1][...] = others
        refs[-2][:, :width], refs[-2][:, width:] = whiten_rows(raw_ref[...], others.astype(jnp.float32), total_bins)

    vmem = pl.BlockSpec(memory_space=pltpu.VMEM)
    return pl.pallas_call(
        body,
        out_shape=[jax.ShapeDtypeStruct(raw.shape, jnp.bfloat16), jax.ShapeDtypeStruct((rows, width), jnp.bfloat16)],
        in_specs=[vmem] * (2 + len(received)),
        out_specs=[vmem, vmem],
        compiler_params=pltpu.CompilerParams(vmem_limit_bytes=6 * 2**20),
        cost_estimate=cost(0.2),
    )(raw, valid, *received)


def whiten_passed(raw, others, total_bins):
    width = others.shape[1]

    def body(raw_ref, others_ref, out_ref):
        out_ref[:, :width], out_ref[:, width:] = whiten_rows(raw_ref[...], others_ref[...].astype(jnp.float32), total_bins)

    vmem = pl.BlockSpec(memory_space=pltpu.VMEM)
    return pl.pallas_call(
        body,
        out_shape=jax.ShapeDtypeStruct(raw.shape, jnp.bfloat16),
        in_specs=[vmem, vmem],
        out_specs=vmem,
        compiler_params=pltpu.CompilerParams(vmem_limit_bytes=6 * 2**20),
        cost_estimate=cost(0.2),
    )(raw, others)


def select(numbers, first):
    wanted = numbers - first
    return (wanted == lax.broadcasted_iota(jnp.int32, wanted.shape, 1)).astype(jnp.bfloat16)


def pick(block, numbers, places):
    def body(block_ref, numbers_ref, out_ref):
        selector = select(numbers_ref[...], places()[0] * block_ref.shape[0])
        out_ref[...] = jnp.dot(selector, block_ref[...], preferred_element_type=jnp.float32).astype(jnp.bfloat16)

    vmem = pl.BlockSpec(memory_space=pltpu.VMEM)
    return pl.pallas_call(
        body,
        out_shape=jax.ShapeDtypeStruct((numbers.shape[0], block.shape[1]), jnp.bfloat16),
        in_specs=[vmem, vmem],
        out_specs=vmem,
        compiler_params=pltpu.CompilerParams(vmem_limit_bytes=6 * 2**20),
        cost_estimate=cost(0.1),
    )(block, numbers)


def cross_blocks(left, blocks, places, cross, total, scaling, numbers=None, stations=None, microseconds=0.0):
    rows, depth = left.shape[0] // 2, left.shape[1]
    pieces = [len(block) for block in blocks]
    count = sum(pieces)
    vmem, anywhere = pl.BlockSpec(memory_space=pltpu.VMEM), pl.BlockSpec(memory_space=pl.ANY)
    operands = [left, *(piece for block in blocks for piece in block)]
    specs = [vmem] * len(operands)
    for more in (numbers, stations):
        if more is not None:
            operands.append(more)
            specs.append(vmem)
    aliases = {}
    if cross is not None:
        aliases = {len(operands): 0}
        operands.append(cross)
        specs.append(anywhere)
    shapes, out_specs = [jax.ShapeDtypeStruct((2, rows, total), jnp.bfloat16)], [anywhere]
    if numbers is not None:
        shapes.append(jax.ShapeDtypeStruct((numbers.shape[0], depth), jnp.bfloat16))
        out_specs.append(vmem)

    def body(left_ref, *refs):
        held, sems = refs[-2:]
        out_ref = refs[len(operands) - 1]
        copies, picked = [], None
        for k, place in enumerate(places()):
            first = sum(pieces[:k])
            block = jnp.concatenate([ref[...] for ref in refs[first : first + pieces[k]]], axis=0)
            product = lax.dot_general(left_ref[...], block, ROWS_T, preferred_element_type=jnp.float32)
            held[k] = (product * scaling).astype(jnp.bfloat16).reshape(2, rows, rows)
            start = pl.multiple_of(place * rows, rows)
            copies.append(pltpu.make_async_copy(held.at[k], out_ref.at[:, :, pl.ds(start, rows)], sems.at[k]))
            copies[k].start()
            if numbers is not None:
                found = jnp.dot(select(refs[count][...], start), block, preferred_element_type=jnp.float32)
                picked = found if picked is None else picked + found
        if numbers is not None:
            if stations is not None:
                picked = picked + refs[count + 1][...].astype(jnp.float32)
            refs[len(operands)][...] = picked.astype(jnp.bfloat16)
        for copy in copies:
            copy.wait()

    out = pl.pallas_call(
        body,
        out_shape=shapes,
        in_specs=specs,
        out_specs=out_specs,
        scratch_shapes=[
            pltpu.VMEM((len(blocks), 2, rows, rows), jnp.bfloat16),
            pltpu.SemaphoreType.DMA((len(blocks),)),
        ],
        input_output_aliases=aliases,
        compiler_params=pltpu.CompilerParams(vmem_limit_bytes=6 * 2**20),
        cost_estimate=cost(microseconds),
    )(*operands)
    return out if numbers is not None else out[0]


def station_kernel(parts, left, scaling):
    rows, width = left.shape[0] // 2, left.shape[1] // 2
    stations = parts[0].shape[0]

    def body(left_ref, *refs):
        found = sum(ref[...].astype(jnp.float32) for ref in refs[:-1])
        turned = jnp.concatenate([found[:, width:], -found[:, :width]], axis=1)
        both = jnp.concatenate([found, turned], axis=0).astype(jnp.bfloat16)
        refs[-1][...] = lax.dot_general(both, left_ref[:rows, :], ROWS_T, preferred_element_type=jnp.float32) * scaling

    vmem = pl.BlockSpec(memory_space=pltpu.VMEM)
    return pl.pallas_call(
        body,
        out_shape=jax.ShapeDtypeStruct((2 * stations, rows), jnp.float32),
        in_specs=[vmem] * (1 + len(parts)),
        out_specs=vmem,
        compiler_params=pltpu.CompilerParams(vmem_limit_bytes=6 * 2**20),
        cost_estimate=cost(0.2),
    )(left, *parts)


def spread(table, stations):
    parts, lags = table.shape
    high = lax.reduce_precision(table, 8, 7)
    low = table - high
    same = jnp.eye(stations, dtype=jnp.float32)[None, :, :, None]

    def blocks(values):
        return (values[:, None, None, :] * same).reshape(parts * stations, stations * lags).astype(jnp.bfloat16)

    return jnp.concatenate([blocks(high), blocks(low), blocks(high)], axis=0)


def lag_sums(kernels, table):
    rows = kernels[0].shape[1]
    stations = kernels[0].shape[0] // 2
    lags = table.shape[1] // stations
    groups = 4
    each = stations // groups

    def body(table_ref, *refs):
        out_ref, held, sems = refs[-3:]
        parts = jnp.concatenate([ref[...] for ref in refs[:-3]], axis=0)
        high = parts.astype(jnp.bfloat16).astype(jnp.float32)
        columns = jnp.concatenate([high, high, parts - high], axis=0).T.astype(jnp.bfloat16)
        copies = []
        for group in range(groups):
            part = slice(group * each * lags, (group + 1) * each * lags)
            sums = jnp.dot(columns, table_ref[:, part], preferred_element_type=jnp.float32)
            for k in range(each):
                held[group * each + k] = sums[:, k * lags : (k + 1) * lags]
            part = pl.ds(group * each, each)
            copies.append(pltpu.make_async_copy(held.at[part], out_ref.at[part], sems.at[group]))
            copies[group].start()
        for copy in copies:
            copy.wait()

    vmem = pl.BlockSpec(memory_space=pltpu.VMEM)
    return pl.pallas_call(
        body,
        out_shape=jax.ShapeDtypeStruct((stations, rows, lags), jnp.float32),
        in_specs=[vmem] * (1 + len(kernels)),
        out_specs=pl.BlockSpec(memory_space=pl.ANY),
        scratch_shapes=[pltpu.VMEM((stations, rows, lags), jnp.float32), pltpu.SemaphoreType.DMA((groups,))],
        compiler_params=pltpu.CompilerParams(vmem_limit_bytes=8 * 2**20),
        cost_estimate=cost(8.0),
    )(table, *kernels)


def make_on_device(group_size, freq_size):
    chips = group_size // 2
    ring = ring_pairs(group_size)
    across = [
        (device, device_of(place_of(device, chips) - 1 + 2 * (device % 2), 1 - device % 2, chips)) for device in range(group_size)
    ]

    def swap_by(bit):
        return [(g, g ^ bit) for g in range(group_size)]

    def swap_pieces(block, pieces):
        rows = block.shape[0] // pieces
        return [lax.ppermute(block[k * rows : (k + 1) * rows], "grp", swap_by(1)) for k in range(pieces)]

    def swap(block):
        return swap_pieces(block, 2)

    def from_freq(shift):
        return [(f, (f + shift) % freq_size) for f in range(freq_size)]

    def on_device(spectra, valid, station_index):
        bin_count, chan_count, double_width = spectra.shape
        assert bin_count == 1
        window_count = double_width // 2
        freq_index = lax.axis_index("freq")
        total_chans = chan_count * group_size
        total_bins = bin_count * freq_size
        scaling = 1.0 / math.sqrt(window_count)

        station_count = station_index.shape[0]
        lags_here = LAGS // freq_size
        lag_values = (freq_index * lags_here + jnp.arange(lags_here, dtype=jnp.int32)).astype(jnp.float32)
        tables = []
        for shift in range(freq_size):
            bin_value = lax.rem(freq_index - shift + freq_size, freq_size).astype(jnp.float32) + 1.0
            phase = math.pi * bin_value * lag_values / LAGS
            tables += [jnp.cos(phase), -jnp.sin(phase)]
        table = spread(jnp.stack(tables) / math.sqrt(total_bins), station_count)

        raw, power = band_power(spectra[0])
        valid, numbers = prepare(valid, station_index, raw)
        received = [lax.ppermute(power, "freq", from_freq(shift)) for shift in range(1, freq_size)]
        raw_flying = lax.ppermute(raw, "grp", ring)
        whitened, others = whiten_own(raw, valid, received, total_bins)
        others_flying = lax.ppermute(others, "grp", ring)
        swapped = swap(whitened)
        flying = [None, lax.ppermute(jnp.concatenate(swapped, axis=0), "grp", ring)]
        left = jnp.concatenate(
            [whitened, jnp.concatenate([whitened[:, window_count:], -whitened[:, :window_count]], axis=1)], axis=0
        )
        cross, stations = cross_blocks(
            left, [[whitened], swapped], own_blocks, None, total_chans, scaling, numbers, None, 4.0
        )
        flying[0] = whiten_passed(raw_flying, others_flying, total_bins)

        steps = chips - 1
        waiting, ahead, kernels = [], [], []
        for step in range(steps):
            arrived, cross, stations, swapped, ahead, kernels = lax.optimization_barrier(
                (flying[step], cross, stations, swapped, ahead, kernels)
            )
            if step + 2 < steps:
                flying.append(lax.ppermute(arrived, "grp", ring))
            if step + 3 == steps:
                found = pick(arrived, numbers, functools.partial(ring_blocks, step, chips))
                ahead = [lax.ppermute(lax.ppermute(found, "grp", swap_by(1)), "grp", across)]
            if step == 2:
                table, cross = lax.optimization_barrier((table, cross))
            if step + 2 == steps:
                ahead.append(lax.ppermute(ahead[0], "grp", swap_by(1)))
            next_swapped = swap(arrived)
            if waiting and step + 1 < steps:
                cross, stations = cross_blocks(left, [waiting, swapped], places, cross, total_chans, scaling, numbers, stations)
            waiting, swapped, places = [arrived], next_swapped, functools.partial(ring_blocks, step, chips)
            if step + 2 == steps:
                cross, stations = cross_blocks(left, [waiting, swapped], places, cross, total_chans, scaling, numbers, stations)
                kernels = [station_kernel([stations, *ahead], left, scaling)]
                others = [lax.ppermute(kernels[0], "freq", from_freq(shift)) for shift in range(1, freq_size)]
        station_gather = lag_sums(kernels + others, table)
        cross = cross_blocks(left, [waiting, swapped], places, cross, total_chans, scaling)
        return (cross[None], station_gather)

    return on_device


def solution(mesh):
    placed = (P("freq", "grp", None), P("grp", None), P())
    return jax.shard_map(
        make_on_device(mesh.shape["grp"], mesh.shape["freq"]),
        mesh=mesh,
        in_specs=placed,
        out_specs=(P("freq", None, "grp", None), P(None, "grp", "freq")),
        check_vma=False,
    )
```

```python
import functools
import math

import jax
import jax.numpy as jnp
from jax import lax
from jax.experimental import pallas as pl
from jax.experimental.pallas import tpu as pltpu
from jax.sharding import PartitionSpec as P

LAGS = 256
ROWS_T = (((1,), (1,)), ((), ()))


def device_of(place, core, chips):
    place %= chips
    z, x = (place, 0) if place < chips // 2 else (chips - 1 - place, 1)
    return z * 4 + x * 2 + core


def place_of(device, chips):
    z, x = device // 4, device // 2 % 2
    return z if x == 0 else chips - 1 - z


def ring_pairs(group_size):
    chips = group_size // 2
    return [
        (device, device_of(place_of(device, chips) + 1 - 2 * (device % 2), device % 2, chips)) for device in range(group_size)
    ]


def block_of(place, core, chips):
    place = lax.rem(place + chips, chips)
    half = chips // 2
    return jnp.where(place < half, place * 4, (chips - 1 - place) * 4 + 2) + core


def own_blocks():
    group_index = lax.axis_index("grp")
    return [group_index, group_index + 1 - 2 * lax.rem(group_index, 2)]


def ring_blocks(step, chips):
    group_index = lax.axis_index("grp")
    core = lax.rem(group_index, 2)
    z, x = group_index // 4, lax.rem(group_index // 2, 2)
    place = jnp.where(x == 0, z, chips - 1 - z)
    back = (step // 2 + 1) * (1 - 2 * core)
    kept = core if step % 2 == 0 else 1 - core
    return [block_of(place - back, kept, chips), block_of(place + back, 1 - kept, chips)]


def cost(microseconds):
    return pl.CostEstimate(flops=int(microseconds * 1.15e9), bytes_accessed=0, transcendentals=0)


def band_power(raw):
    rows, width = raw.shape[0], raw.shape[1] // 2

    def body(raw_ref, raw_out, power_out):
        part = raw_ref[...].astype(jnp.float32)
        power_out[...] = (part[:, :width] * part[:, :width] + part[:, width:] * part[:, width:]).astype(jnp.bfloat16)
        raw_out[...] = raw_ref[...]

    vmem = pl.BlockSpec(memory_space=pltpu.VMEM)
    return pl.pallas_call(
        body,
        out_shape=[jax.ShapeDtypeStruct(raw.shape, jnp.bfloat16), jax.ShapeDtypeStruct((rows, width), jnp.bfloat16)],
        in_specs=[vmem],
        out_specs=[vmem, vmem],
        compiler_params=pltpu.CompilerParams(vmem_limit_bytes=6 * 2**20),
        cost_estimate=cost(0.1),
    )(raw)


def prepare(valid, station_index, after):
    rows, width = valid.shape
    stations = station_index.shape[0]

    def body(index_ref, valid_ref, _, valid_out, numbers_out, valid_held, index_held, sems):
        copies = [
            pltpu.make_async_copy(valid_ref, valid_held, sems.at[0]),
            pltpu.make_async_copy(index_ref, index_held, sems.at[1]),
        ]
        for copy in copies:
            copy.start()
        copies[1].wait()
        place = lax.broadcasted_iota(jnp.int32, (stations, rows), 0)
        numbers = jnp.zeros((stations, rows), jnp.int32)
        for k in range(stations):
            numbers = jnp.where(place == k, index_held[k], numbers)
        numbers_out[...] = numbers
        copies[0].wait()
        valid_out[...] = valid_held[...].astype(jnp.bfloat16)

    vmem, anywhere = pl.BlockSpec(memory_space=pltpu.VMEM), pl.BlockSpec(memory_space=pl.ANY)
    return pl.pallas_call(
        body,
        out_shape=[jax.ShapeDtypeStruct(valid.shape, jnp.bfloat16), jax.ShapeDtypeStruct((stations, rows), jnp.int32)],
        in_specs=[anywhere] * 3,
        out_specs=[vmem] * 2,
        scratch_shapes=[
            pltpu.VMEM(valid.shape, jnp.int32),
            pltpu.SMEM(station_index.shape, jnp.int32),
            pltpu.SemaphoreType.DMA((2,)),
        ],
        compiler_params=pltpu.CompilerParams(vmem_limit_bytes=6 * 2**20),
        cost_estimate=cost(0.3),
    )(station_index, valid, after)


def whiten_rows(raw, others, total_bins):
    part = raw.astype(jnp.float32)
    width = part.shape[1] // 2
    real, imag = part[:, :width], part[:, width:]
    power = real * real + imag * imag + others
    factor = jnp.where(others < 0.0, 0.0, lax.rsqrt(power / total_bins + 1e-05))
    return (real * factor).astype(jnp.bfloat16), (imag * factor).astype(jnp.bfloat16)


def whiten_own(raw, valid, received, total_bins):
    rows, width = valid.shape

    def body(raw_ref, valid_ref, *refs):
        others = sum(ref[...].astype(jnp.float32) for ref in refs[:-2])
        others = jnp.where(valid_ref[...].astype(jnp.float32) > 0.0, others, -1.0).astype(jnp.bfloat16)
        refs[-1][...] = others
        refs[-2][:, :width], refs[-2][:, width:] = whiten_rows(raw_ref[...], others.astype(jnp.float32), total_bins)

    vmem = pl.BlockSpec(memory_space=pltpu.VMEM)
    return pl.pallas_call(
        body,
        out_shape=[jax.ShapeDtypeStruct(raw.shape, jnp.bfloat16), jax.ShapeDtypeStruct((rows, width), jnp.bfloat16)],
        in_specs=[vmem] * (2 + len(received)),
        out_specs=[vmem, vmem],
        compiler_params=pltpu.CompilerParams(vmem_limit_bytes=6 * 2**20),
        cost_estimate=cost(0.2),
    )(raw, valid, *received)


def whiten_passed(raw, others, total_bins):
    width = others.shape[1]

    def body(raw_ref, others_ref, out_ref):
        out_ref[:, :width], out_ref[:, width:] = whiten_rows(raw_ref[...], others_ref[...].astype(jnp.float32), total_bins)

    vmem = pl.BlockSpec(memory_space=pltpu.VMEM)
    return pl.pallas_call(
        body,
        out_shape=jax.ShapeDtypeStruct(raw.shape, jnp.bfloat16),
        in_specs=[vmem, vmem],
        out_specs=vmem,
        compiler_params=pltpu.CompilerParams(vmem_limit_bytes=6 * 2**20),
        cost_estimate=cost(0.2),
    )(raw, others)


def select(numbers, first):
    wanted = numbers - first
    return (wanted == lax.broadcasted_iota(jnp.int32, wanted.shape, 1)).astype(jnp.bfloat16)


def pick(blocks, numbers, places):
    rows, depth = sum(piece.shape[0] for piece in blocks[0]), blocks[0][0].shape[1]
    pieces = [len(block) for block in blocks]

    def body(numbers_ref, *refs):
        picked = None
        for k, place in enumerate(places()[: len(blocks)]):
            first = sum(pieces[:k])
            block = jnp.concatenate([ref[...] for ref in refs[first : first + pieces[k]]], axis=0)
            found = jnp.dot(select(numbers_ref[...], place * rows), block, preferred_element_type=jnp.float32)
            picked = found if picked is None else picked + found
        refs[-1][...] = picked.astype(jnp.bfloat16)

    vmem = pl.BlockSpec(memory_space=pltpu.VMEM)
    return pl.pallas_call(
        body,
        out_shape=jax.ShapeDtypeStruct((numbers.shape[0], depth), jnp.bfloat16),
        in_specs=[vmem] * (1 + sum(pieces)),
        out_specs=vmem,
        compiler_params=pltpu.CompilerParams(vmem_limit_bytes=6 * 2**20),
        cost_estimate=cost(0.1),
    )(numbers, *(piece for block in blocks for piece in block))


def cross_blocks(left, blocks, places, cross, total, scaling, numbers=None, stations=None, microseconds=0.0):
    rows, depth = left.shape[0] // 2, left.shape[1]
    pieces = [len(block) for block in blocks]
    count = sum(pieces)
    vmem, anywhere = pl.BlockSpec(memory_space=pltpu.VMEM), pl.BlockSpec(memory_space=pl.ANY)
    operands = [left, *(piece for block in blocks for piece in block)]
    specs = [vmem] * len(operands)
    for more in (numbers, stations):
        if more is not None:
            operands.append(more)
            specs.append(vmem)
    aliases = {}
    if cross is not None:
        aliases = {len(operands): 0}
        operands.append(cross)
        specs.append(anywhere)
    shapes, out_specs = [jax.ShapeDtypeStruct((2, rows, total), jnp.bfloat16)], [anywhere]
    if numbers is not None:
        shapes.append(jax.ShapeDtypeStruct((numbers.shape[0], depth), jnp.bfloat16))
        out_specs.append(vmem)

    def body(left_ref, *refs):
        held, sems = refs[-2:]
        out_ref = refs[len(operands) - 1]
        copies, picked = [], None
        for k, place in enumerate(places()):
            first = sum(pieces[:k])
            block = jnp.concatenate([ref[...] for ref in refs[first : first + pieces[k]]], axis=0)
            product = lax.dot_general(left_ref[...], block, ROWS_T, preferred_element_type=jnp.float32)
            held[k] = (product * scaling).astype(jnp.bfloat16).reshape(2, rows, rows)
            start = pl.multiple_of(place * rows, rows)
            copies.append(pltpu.make_async_copy(held.at[k], out_ref.at[:, :, pl.ds(start, rows)], sems.at[k]))
            copies[k].start()
            if numbers is not None:
                found = jnp.dot(select(refs[count][...], start), block, preferred_element_type=jnp.float32)
                picked = found if picked is None else picked + found
        if numbers is not None:
            if stations is not None:
                picked = picked + refs[count + 1][...].astype(jnp.float32)
            refs[len(operands)][...] = picked.astype(jnp.bfloat16)
        for copy in copies:
            copy.wait()

    out = pl.pallas_call(
        body,
        out_shape=shapes,
        in_specs=specs,
        out_specs=out_specs,
        scratch_shapes=[
            pltpu.VMEM((len(blocks), 2, rows, rows), jnp.bfloat16),
            pltpu.SemaphoreType.DMA((len(blocks),)),
        ],
        input_output_aliases=aliases,
        compiler_params=pltpu.CompilerParams(vmem_limit_bytes=6 * 2**20),
        cost_estimate=cost(microseconds),
    )(*operands)
    return out if numbers is not None else out[0]


def station_kernel(parts, left, scaling):
    rows, width = left.shape[0] // 2, left.shape[1] // 2
    stations = parts[0].shape[0]

    def body(left_ref, *refs):
        found = sum(ref[...].astype(jnp.float32) for ref in refs[:-1])
        turned = jnp.concatenate([found[:, width:], -found[:, :width]], axis=1)
        both = jnp.concatenate([found, turned], axis=0).astype(jnp.bfloat16)
        refs[-1][...] = lax.dot_general(both, left_ref[:rows, :], ROWS_T, preferred_element_type=jnp.float32) * scaling

    vmem = pl.BlockSpec(memory_space=pltpu.VMEM)
    return pl.pallas_call(
        body,
        out_shape=jax.ShapeDtypeStruct((2 * stations, rows), jnp.float32),
        in_specs=[vmem] * (1 + len(parts)),
        out_specs=vmem,
        compiler_params=pltpu.CompilerParams(vmem_limit_bytes=6 * 2**20),
        cost_estimate=cost(0.2),
    )(left, *parts)


def spread(table, stations):
    parts, lags = table.shape
    high = lax.reduce_precision(table, 8, 7)
    low = table - high
    same = jnp.eye(stations, dtype=jnp.float32)[None, :, :, None]

    def blocks(values):
        return (values[:, None, None, :] * same).reshape(parts * stations, stations * lags).astype(jnp.bfloat16)

    return jnp.concatenate([blocks(high), blocks(low), blocks(high)], axis=0)


def lag_sums(kernels, table):
    rows = kernels[0].shape[1]
    stations = kernels[0].shape[0] // 2
    lags = table.shape[1] // stations
    groups = 4
    each = stations // groups

    def body(table_ref, *refs):
        out_ref, held, sems = refs[-3:]
        parts = jnp.concatenate([ref[...] for ref in refs[:-3]], axis=0)
        high = parts.astype(jnp.bfloat16).astype(jnp.float32)
        columns = jnp.concatenate([high, high, parts - high], axis=0).T.astype(jnp.bfloat16)
        copies = []
        for group in range(groups):
            part = slice(group * each * lags, (group + 1) * each * lags)
            sums = jnp.dot(columns, table_ref[:, part], preferred_element_type=jnp.float32)
            for k in range(each):
                held[group * each + k] = sums[:, k * lags : (k + 1) * lags]
            part = pl.ds(group * each, each)
            copies.append(pltpu.make_async_copy(held.at[part], out_ref.at[part], sems.at[group]))
            copies[group].start()
        for copy in copies:
            copy.wait()

    vmem = pl.BlockSpec(memory_space=pltpu.VMEM)
    return pl.pallas_call(
        body,
        out_shape=jax.ShapeDtypeStruct((stations, rows, lags), jnp.float32),
        in_specs=[vmem] * (1 + len(kernels)),
        out_specs=pl.BlockSpec(memory_space=pl.ANY),
        scratch_shapes=[pltpu.VMEM((stations, rows, lags), jnp.float32), pltpu.SemaphoreType.DMA((groups,))],
        compiler_params=pltpu.CompilerParams(vmem_limit_bytes=8 * 2**20),
        cost_estimate=cost(8.0),
    )(table, *kernels)


def make_on_device(group_size, freq_size):
    chips = group_size // 2
    ring = ring_pairs(group_size)
    across = [
        (device, device_of(place_of(device, chips) - 1 + 2 * (device % 2), 1 - device % 2, chips)) for device in range(group_size)
    ]

    def swap_by(bit):
        return [(g, g ^ bit) for g in range(group_size)]

    def swap_pieces(block, pieces):
        rows = block.shape[0] // pieces
        return [lax.ppermute(block[k * rows : (k + 1) * rows], "grp", swap_by(1)) for k in range(pieces)]

    def swap(block):
        return swap_pieces(block, 2)

    def from_freq(shift):
        return [(f, (f + shift) % freq_size) for f in range(freq_size)]

    def on_device(spectra, valid, station_index):
        bin_count, chan_count, double_width = spectra.shape
        assert bin_count == 1
        window_count = double_width // 2
        freq_index = lax.axis_index("freq")
        total_chans = chan_count * group_size
        total_bins = bin_count * freq_size
        scaling = 1.0 / math.sqrt(window_count)

        station_count = station_index.shape[0]
        lags_here = LAGS // freq_size
        lag_values = (freq_index * lags_here + jnp.arange(lags_here, dtype=jnp.int32)).astype(jnp.float32)
        tables = []
        for shift in range(freq_size):
            bin_value = lax.rem(freq_index - shift + freq_size, freq_size).astype(jnp.float32) + 1.0
            phase = math.pi * bin_value * lag_values / LAGS
            tables += [jnp.cos(phase), -jnp.sin(phase)]
        table = spread(jnp.stack(tables) / math.sqrt(total_bins), station_count)

        raw, power = band_power(spectra[0])
        valid, numbers = prepare(valid, station_index, raw)
        received = [lax.ppermute(power, "freq", from_freq(shift)) for shift in range(1, freq_size)]
        raw_flying = lax.ppermute(raw, "grp", ring)
        whitened, others = whiten_own(raw, valid, received, total_bins)
        others_flying = lax.ppermute(others, "grp", ring)
        swapped = swap(whitened)
        flying = [None, lax.ppermute(jnp.concatenate(swapped, axis=0), "grp", ring)]
        left = jnp.concatenate(
            [whitened, jnp.concatenate([whitened[:, window_count:], -whitened[:, :window_count]], axis=1)], axis=0
        )
        cross, stations = cross_blocks(
            left, [[whitened], swapped], own_blocks, None, total_chans, scaling, numbers, None, 4.0
        )
        flying[0] = whiten_passed(raw_flying, others_flying, total_bins)

        steps = chips - 1
        waiting, ahead, kernels = [], [], []
        for step in range(steps):
            arrived, cross, stations, swapped, ahead, kernels = lax.optimization_barrier(
                (flying[step], cross, stations, swapped, ahead, kernels)
            )
            if step + 2 < steps:
                flying.append(lax.ppermute(arrived, "grp", ring))
            if step + 3 == steps:
                found = pick([[arrived]], numbers, functools.partial(ring_blocks, step, chips))
                ahead = [lax.ppermute(lax.ppermute(found, "grp", swap_by(1)), "grp", across)]
            if step == 2:
                table, cross = lax.optimization_barrier((table, cross))
            if step + 2 == steps:
                ahead.append(lax.ppermute(ahead[0], "grp", swap_by(1)))
            next_swapped = swap(arrived)
            if waiting and step + 1 < steps:
                cross, stations = cross_blocks(left, [waiting, swapped], places, cross, total_chans, scaling, numbers, stations)
            waiting, swapped, places = [arrived], next_swapped, functools.partial(ring_blocks, step, chips)
            if step + 2 == steps:
                found = pick([waiting, swapped], numbers, places)
                kernels = [station_kernel([stations, found, *ahead], left, scaling)]
                others = [lax.ppermute(kernels[0], "freq", from_freq(shift)) for shift in range(1, freq_size)]
                cross, kernels = lax.optimization_barrier((cross, kernels))
                cross = cross_blocks(left, [waiting, swapped], places, cross, total_chans, scaling)
        station_gather = lag_sums(kernels + others, table)
        cross = cross_blocks(left, [waiting, swapped], places, cross, total_chans, scaling)
        return (cross[None], station_gather)

    return on_device


def solution(mesh):
    placed = (P("freq", "grp", None), P("grp", None), P())
    return jax.shard_map(
        make_on_device(mesh.shape["grp"], mesh.shape["freq"]),
        mesh=mesh,
        in_specs=placed,
        out_specs=(P("freq", None, "grp", None), P(None, "grp", "freq")),
        check_vma=False,
    )
```

```python
import functools
import math

import jax
import jax.numpy as jnp
from jax import lax
from jax.experimental import pallas as pl
from jax.experimental.pallas import tpu as pltpu
from jax.sharding import PartitionSpec as P

LAGS = 256
ROWS_T = (((1,), (1,)), ((), ()))


def device_of(place, core, chips):
    place %= chips
    z, x = (place, 0) if place < chips // 2 else (chips - 1 - place, 1)
    return z * 4 + x * 2 + core


def place_of(device, chips):
    z, x = device // 4, device // 2 % 2
    return z if x == 0 else chips - 1 - z


def ring_pairs(group_size):
    chips = group_size // 2
    return [
        (device, device_of(place_of(device, chips) + 1 - 2 * (device % 2), device % 2, chips)) for device in range(group_size)
    ]


def block_of(place, core, chips):
    place = lax.rem(place + chips, chips)
    half = chips // 2
    return jnp.where(place < half, place * 4, (chips - 1 - place) * 4 + 2) + core


def own_blocks():
    group_index = lax.axis_index("grp")
    return [group_index, group_index + 1 - 2 * lax.rem(group_index, 2)]


def ring_blocks(step, chips):
    group_index = lax.axis_index("grp")
    core = lax.rem(group_index, 2)
    z, x = group_index // 4, lax.rem(group_index // 2, 2)
    place = jnp.where(x == 0, z, chips - 1 - z)
    back = (step // 2 + 1) * (1 - 2 * core)
    kept = core if step % 2 == 0 else 1 - core
    return [block_of(place - back, kept, chips), block_of(place + back, 1 - kept, chips)]


def cost(microseconds):
    return pl.CostEstimate(flops=int(microseconds * 1.15e9), bytes_accessed=0, transcendentals=0)


def band_power(raw):
    rows, width = raw.shape[0], raw.shape[1] // 2

    def body(raw_ref, raw_out, power_out):
        part = raw_ref[...].astype(jnp.float32)
        power_out[...] = (part[:, :width] * part[:, :width] + part[:, width:] * part[:, width:]).astype(jnp.bfloat16)
        raw_out[...] = raw_ref[...]

    vmem = pl.BlockSpec(memory_space=pltpu.VMEM)
    return pl.pallas_call(
        body,
        out_shape=[jax.ShapeDtypeStruct(raw.shape, jnp.bfloat16), jax.ShapeDtypeStruct((rows, width), jnp.bfloat16)],
        in_specs=[vmem],
        out_specs=[vmem, vmem],
        compiler_params=pltpu.CompilerParams(vmem_limit_bytes=6 * 2**20),
        cost_estimate=cost(0.1),
    )(raw)


def prepare(valid, station_index, after):
    rows, width = valid.shape
    stations = station_index.shape[0]

    def body(index_ref, valid_ref, _, valid_out, numbers_out, valid_held, index_held, sems):
        copies = [
            pltpu.make_async_copy(valid_ref, valid_held, sems.at[0]),
            pltpu.make_async_copy(index_ref, index_held, sems.at[1]),
        ]
        for copy in copies:
            copy.start()
        copies[1].wait()
        place = lax.broadcasted_iota(jnp.int32, (stations, rows), 0)
        numbers = jnp.zeros((stations, rows), jnp.int32)
        for k in range(stations):
            numbers = jnp.where(place == k, index_held[k], numbers)
        numbers_out[...] = numbers
        copies[0].wait()
        valid_out[...] = valid_held[...].astype(jnp.bfloat16)

    vmem, anywhere = pl.BlockSpec(memory_space=pltpu.VMEM), pl.BlockSpec(memory_space=pl.ANY)
    return pl.pallas_call(
        body,
        out_shape=[jax.ShapeDtypeStruct(valid.shape, jnp.bfloat16), jax.ShapeDtypeStruct((stations, rows), jnp.int32)],
        in_specs=[anywhere] * 3,
        out_specs=[vmem] * 2,
        scratch_shapes=[
            pltpu.VMEM(valid.shape, jnp.int32),
            pltpu.SMEM(station_index.shape, jnp.int32),
            pltpu.SemaphoreType.DMA((2,)),
        ],
        compiler_params=pltpu.CompilerParams(vmem_limit_bytes=6 * 2**20),
        cost_estimate=cost(0.3),
    )(station_index, valid, after)


def whiten_rows(raw, others, total_bins):
    part = raw.astype(jnp.float32)
    width = part.shape[1] // 2
    real, imag = part[:, :width], part[:, width:]
    power = real * real + imag * imag + others
    factor = jnp.where(others < 0.0, 0.0, lax.rsqrt(power / total_bins + 1e-05))
    return (real * factor).astype(jnp.bfloat16), (imag * factor).astype(jnp.bfloat16)


def whiten_own(raw, valid, received, total_bins):
    rows, width = valid.shape

    def body(raw_ref, valid_ref, *refs):
        others = sum(ref[...].astype(jnp.float32) for ref in refs[:-2])
        others = jnp.where(valid_ref[...].astype(jnp.float32) > 0.0, others, -1.0).astype(jnp.bfloat16)
        refs[-1][...] = others
        refs[-2][:, :width], refs[-2][:, width:] = whiten_rows(raw_ref[...], others.astype(jnp.float32), total_bins)

    vmem = pl.BlockSpec(memory_space=pltpu.VMEM)
    return pl.pallas_call(
        body,
        out_shape=[jax.ShapeDtypeStruct(raw.shape, jnp.bfloat16), jax.ShapeDtypeStruct((rows, width), jnp.bfloat16)],
        in_specs=[vmem] * (2 + len(received)),
        out_specs=[vmem, vmem],
        compiler_params=pltpu.CompilerParams(vmem_limit_bytes=6 * 2**20),
        cost_estimate=cost(0.2),
    )(raw, valid, *received)


def whiten_passed(raw, others, total_bins):
    width = others.shape[1]

    def body(raw_ref, others_ref, out_ref):
        out_ref[:, :width], out_ref[:, width:] = whiten_rows(raw_ref[...], others_ref[...].astype(jnp.float32), total_bins)

    vmem = pl.BlockSpec(memory_space=pltpu.VMEM)
    return pl.pallas_call(
        body,
        out_shape=jax.ShapeDtypeStruct(raw.shape, jnp.bfloat16),
        in_specs=[vmem, vmem],
        out_specs=vmem,
        compiler_params=pltpu.CompilerParams(vmem_limit_bytes=6 * 2**20),
        cost_estimate=cost(0.2),
    )(raw, others)


def select(numbers, first):
    wanted = numbers - first
    return (wanted == lax.broadcasted_iota(jnp.int32, wanted.shape, 1)).astype(jnp.bfloat16)


def pick(blocks, numbers, places):
    rows, depth = sum(piece.shape[0] for piece in blocks[0]), blocks[0][0].shape[1]
    pieces = [len(block) for block in blocks]

    def body(numbers_ref, *refs):
        picked = None
        for k, place in enumerate(places()[: len(blocks)]):
            first = sum(pieces[:k])
            block = jnp.concatenate([ref[...] for ref in refs[first : first + pieces[k]]], axis=0)
            found = jnp.dot(select(numbers_ref[...], place * rows), block, preferred_element_type=jnp.float32)
            picked = found if picked is None else picked + found
        refs[-1][...] = picked.astype(jnp.bfloat16)

    vmem = pl.BlockSpec(memory_space=pltpu.VMEM)
    return pl.pallas_call(
        body,
        out_shape=jax.ShapeDtypeStruct((numbers.shape[0], depth), jnp.bfloat16),
        in_specs=[vmem] * (1 + sum(pieces)),
        out_specs=vmem,
        compiler_params=pltpu.CompilerParams(vmem_limit_bytes=6 * 2**20),
        cost_estimate=cost(0.1),
    )(numbers, *(piece for block in blocks for piece in block))


def cross_blocks(left, blocks, places, cross, total, scaling, numbers=None, stations=None, microseconds=0.0):
    rows, depth = left.shape[0] // 2, left.shape[1]
    pieces = [len(block) for block in blocks]
    count = sum(pieces)
    vmem, anywhere = pl.BlockSpec(memory_space=pltpu.VMEM), pl.BlockSpec(memory_space=pl.ANY)
    operands = [left, *(piece for block in blocks for piece in block)]
    specs = [vmem] * len(operands)
    for more in (numbers, stations):
        if more is not None:
            operands.append(more)
            specs.append(vmem)
    aliases = {}
    if cross is not None:
        aliases = {len(operands): 0}
        operands.append(cross)
        specs.append(anywhere)
    shapes, out_specs = [jax.ShapeDtypeStruct((2, rows, total), jnp.bfloat16)], [anywhere]
    if numbers is not None:
        shapes.append(jax.ShapeDtypeStruct((numbers.shape[0], depth), jnp.bfloat16))
        out_specs.append(vmem)

    def body(left_ref, *refs):
        held, sems = refs[-2:]
        out_ref = refs[len(operands) - 1]
        copies, picked = [], None
        for k, place in enumerate(places()):
            first = sum(pieces[:k])
            block = jnp.concatenate([ref[...] for ref in refs[first : first + pieces[k]]], axis=0)
            product = lax.dot_general(left_ref[...], block, ROWS_T, preferred_element_type=jnp.float32)
            held[k] = (product * scaling).astype(jnp.bfloat16).reshape(2, rows, rows)
            start = pl.multiple_of(place * rows, rows)
            copies.append(pltpu.make_async_copy(held.at[k], out_ref.at[:, :, pl.ds(start, rows)], sems.at[k]))
            copies[k].start()
            if numbers is not None:
                found = jnp.dot(select(refs[count][...], start), block, preferred_element_type=jnp.float32)
                picked = found if picked is None else picked + found
        if numbers is not None:
            if stations is not None:
                picked = picked + refs[count + 1][...].astype(jnp.float32)
            refs[len(operands)][...] = picked.astype(jnp.bfloat16)
        for copy in copies:
            copy.wait()

    out = pl.pallas_call(
        body,
        out_shape=shapes,
        in_specs=specs,
        out_specs=out_specs,
        scratch_shapes=[
            pltpu.VMEM((len(blocks), 2, rows, rows), jnp.bfloat16),
            pltpu.SemaphoreType.DMA((len(blocks),)),
        ],
        input_output_aliases=aliases,
        compiler_params=pltpu.CompilerParams(vmem_limit_bytes=6 * 2**20),
        cost_estimate=cost(microseconds),
    )(*operands)
    return out if numbers is not None else out[0]


def station_kernel(parts, left, scaling):
    rows, width = left.shape[0] // 2, left.shape[1] // 2
    stations = parts[0].shape[0]

    def body(left_ref, *refs):
        found = sum(ref[...].astype(jnp.float32) for ref in refs[:-1])
        turned = jnp.concatenate([found[:, width:], -found[:, :width]], axis=1)
        both = jnp.concatenate([found, turned], axis=0).astype(jnp.bfloat16)
        refs[-1][...] = lax.dot_general(both, left_ref[:rows, :], ROWS_T, preferred_element_type=jnp.float32) * scaling

    vmem = pl.BlockSpec(memory_space=pltpu.VMEM)
    return pl.pallas_call(
        body,
        out_shape=jax.ShapeDtypeStruct((2 * stations, rows), jnp.float32),
        in_specs=[vmem] * (1 + len(parts)),
        out_specs=vmem,
        compiler_params=pltpu.CompilerParams(vmem_limit_bytes=6 * 2**20),
        cost_estimate=cost(0.2),
    )(left, *parts)


def spread(table, stations):
    parts, lags = table.shape
    high = lax.reduce_precision(table, 8, 7)
    low = table - high
    same = jnp.eye(stations, dtype=jnp.float32)[None, :, :, None]

    def blocks(values):
        return (values[:, None, None, :] * same).reshape(parts * stations, stations * lags).astype(jnp.bfloat16)

    return jnp.concatenate([blocks(high), blocks(low), blocks(high)], axis=0)


def lag_sums(kernels, table):
    rows = kernels[0].shape[1]
    stations = kernels[0].shape[0] // 2
    lags = table.shape[1] // stations
    groups = 4
    each = stations // groups

    def body(table_ref, *refs):
        out_ref, held, sems = refs[-3:]
        parts = jnp.concatenate([ref[...] for ref in refs[:-3]], axis=0)
        high = parts.astype(jnp.bfloat16).astype(jnp.float32)
        columns = jnp.concatenate([high, high, parts - high], axis=0).T.astype(jnp.bfloat16)
        copies = []
        for group in range(groups):
            part = slice(group * each * lags, (group + 1) * each * lags)
            sums = jnp.dot(columns, table_ref[:, part], preferred_element_type=jnp.float32)
            for k in range(each):
                held[group * each + k] = sums[:, k * lags : (k + 1) * lags]
            part = pl.ds(group * each, each)
            copies.append(pltpu.make_async_copy(held.at[part], out_ref.at[part], sems.at[group]))
            copies[group].start()
        for copy in copies:
            copy.wait()

    vmem = pl.BlockSpec(memory_space=pltpu.VMEM)
    return pl.pallas_call(
        body,
        out_shape=jax.ShapeDtypeStruct((stations, rows, lags), jnp.float32),
        in_specs=[vmem] * (1 + len(kernels)),
        out_specs=pl.BlockSpec(memory_space=pl.ANY),
        scratch_shapes=[pltpu.VMEM((stations, rows, lags), jnp.float32), pltpu.SemaphoreType.DMA((groups,))],
        compiler_params=pltpu.CompilerParams(vmem_limit_bytes=8 * 2**20),
        cost_estimate=cost(8.0),
    )(table, *kernels)


def make_on_device(group_size, freq_size):
    chips = group_size // 2
    ring = ring_pairs(group_size)
    across = [
        (device, device_of(place_of(device, chips) - 1 + 2 * (device % 2), 1 - device % 2, chips)) for device in range(group_size)
    ]

    def swap_by(bit):
        return [(g, g ^ bit) for g in range(group_size)]

    def swap_pieces(block, pieces):
        rows = block.shape[0] // pieces
        return [lax.ppermute(block[k * rows : (k + 1) * rows], "grp", swap_by(1)) for k in range(pieces)]

    def swap(block):
        return swap_pieces(block, 2)

    def from_freq(shift):
        return [(f, (f + shift) % freq_size) for f in range(freq_size)]

    def on_device(spectra, valid, station_index):
        bin_count, chan_count, double_width = spectra.shape
        assert bin_count == 1
        window_count = double_width // 2
        freq_index = lax.axis_index("freq")
        total_chans = chan_count * group_size
        total_bins = bin_count * freq_size
        scaling = 1.0 / math.sqrt(window_count)

        station_count = station_index.shape[0]
        lags_here = LAGS // freq_size
        lag_values = (freq_index * lags_here + jnp.arange(lags_here, dtype=jnp.int32)).astype(jnp.float32)
        tables = []
        for shift in range(freq_size):
            bin_value = lax.rem(freq_index - shift + freq_size, freq_size).astype(jnp.float32) + 1.0
            phase = math.pi * bin_value * lag_values / LAGS
            tables += [jnp.cos(phase), -jnp.sin(phase)]
        table = spread(jnp.stack(tables) / math.sqrt(total_bins), station_count)

        raw, power = band_power(spectra[0])
        valid, numbers = prepare(valid, station_index, raw)
        received = [lax.ppermute(power, "freq", from_freq(shift)) for shift in range(1, freq_size)]
        raw_flying = lax.ppermute(raw, "grp", ring)
        whitened, others = whiten_own(raw, valid, received, total_bins)
        others_flying = lax.ppermute(others, "grp", ring)
        swapped = swap(whitened)
        flying = [None, lax.ppermute(jnp.concatenate(swapped, axis=0), "grp", ring)]
        left = jnp.concatenate(
            [whitened, jnp.concatenate([whitened[:, window_count:], -whitened[:, :window_count]], axis=1)], axis=0
        )
        flying[0] = whiten_passed(raw_flying, others_flying, total_bins)

        steps = chips - 1
        waiting, ahead, kernels = [], [], []
        cross = stations = None
        for step in range(steps):
            arrived, cross, stations, swapped, ahead, kernels = lax.optimization_barrier(
                (flying[step], cross, stations, swapped, ahead, kernels)
            )
            if step + 2 < steps:
                flying.append(lax.ppermute(arrived, "grp", ring))
            if step + 3 == steps:
                found = pick([[arrived]], numbers, functools.partial(ring_blocks, step, chips))
                ahead = [lax.ppermute(lax.ppermute(found, "grp", swap_by(1)), "grp", across)]
            if step == 2:
                table, cross = lax.optimization_barrier((table, cross))
            if step + 2 == steps:
                ahead.append(lax.ppermute(ahead[0], "grp", swap_by(1)))
            next_swapped = swap(arrived)
            if step == 0:
                cross, stations = cross_blocks(
                    left, [[whitened], swapped], own_blocks, None, total_chans, scaling, numbers, None, 4.0
                )
            elif step + 1 < steps:
                cross, stations = cross_blocks(left, [waiting, swapped], places, cross, total_chans, scaling, numbers, stations)
            waiting, swapped, places = [arrived], next_swapped, functools.partial(ring_blocks, step, chips)
            if step + 2 == steps:
                found = pick([waiting, swapped], numbers, places)
                kernels = [station_kernel([stations, found, *ahead], left, scaling)]
                others = [lax.ppermute(kernels[0], "freq", from_freq(shift)) for shift in range(1, freq_size)]
                cross, kernels = lax.optimization_barrier((cross, kernels))
                cross = cross_blocks(left, [waiting, swapped], places, cross, total_chans, scaling)
        station_gather = lag_sums(kernels + others, table)
        cross = cross_blocks(left, [waiting, swapped], places, cross, total_chans, scaling)
        return (cross[None], station_gather)

    return on_device


def solution(mesh):
    placed = (P("freq", "grp", None), P("grp", None), P())
    return jax.shard_map(
        make_on_device(mesh.shape["grp"], mesh.shape["freq"]),
        mesh=mesh,
        in_specs=placed,
        out_specs=(P("freq", None, "grp", None), P(None, "grp", "freq")),
        check_vma=False,
    )
```

```python
import functools
import math

import jax
import jax.numpy as jnp
from jax import lax
from jax.experimental import pallas as pl
from jax.experimental.pallas import tpu as pltpu
from jax.sharding import PartitionSpec as P

LAGS = 256
ROWS_T = (((1,), (1,)), ((), ()))


def device_of(place, core, chips):
    place %= chips
    z, x = (place, 0) if place < chips // 2 else (chips - 1 - place, 1)
    return z * 4 + x * 2 + core


def place_of(device, chips):
    z, x = device // 4, device // 2 % 2
    return z if x == 0 else chips - 1 - z


def ring_pairs(group_size):
    chips = group_size // 2
    return [
        (device, device_of(place_of(device, chips) + 1 - 2 * (device % 2), device % 2, chips)) for device in range(group_size)
    ]


def block_of(place, core, chips):
    place = lax.rem(place + chips, chips)
    half = chips // 2
    return jnp.where(place < half, place * 4, (chips - 1 - place) * 4 + 2) + core


def own_blocks():
    group_index = lax.axis_index("grp")
    return [group_index, group_index + 1 - 2 * lax.rem(group_index, 2)]


def ring_blocks(step, chips):
    group_index = lax.axis_index("grp")
    core = lax.rem(group_index, 2)
    z, x = group_index // 4, lax.rem(group_index // 2, 2)
    place = jnp.where(x == 0, z, chips - 1 - z)
    back = (step // 2 + 1) * (1 - 2 * core)
    kept = core if step % 2 == 0 else 1 - core
    return [block_of(place - back, kept, chips), block_of(place + back, 1 - kept, chips)]


def cost(microseconds):
    return pl.CostEstimate(flops=int(microseconds * 1.15e9), bytes_accessed=0, transcendentals=0)


def band_power(raw):
    rows, width = raw.shape[0], raw.shape[1] // 2

    def body(raw_ref, raw_out, power_out):
        part = raw_ref[...].astype(jnp.float32)
        power_out[...] = (part[:, :width] * part[:, :width] + part[:, width:] * part[:, width:]).astype(jnp.bfloat16)
        raw_out[...] = raw_ref[...]

    vmem = pl.BlockSpec(memory_space=pltpu.VMEM)
    return pl.pallas_call(
        body,
        out_shape=[jax.ShapeDtypeStruct(raw.shape, jnp.bfloat16), jax.ShapeDtypeStruct((rows, width), jnp.bfloat16)],
        in_specs=[vmem],
        out_specs=[vmem, vmem],
        compiler_params=pltpu.CompilerParams(vmem_limit_bytes=6 * 2**20),
        cost_estimate=cost(0.1),
    )(raw)


def prepare(valid, station_index, after):
    rows, width = valid.shape
    stations = station_index.shape[0]

    def body(index_ref, valid_ref, _, valid_out, numbers_out, valid_held, index_held, sems):
        copies = [
            pltpu.make_async_copy(valid_ref, valid_held, sems.at[0]),
            pltpu.make_async_copy(index_ref, index_held, sems.at[1]),
        ]
        for copy in copies:
            copy.start()
        copies[1].wait()
        place = lax.broadcasted_iota(jnp.int32, (stations, rows), 0)
        numbers = jnp.zeros((stations, rows), jnp.int32)
        for k in range(stations):
            numbers = jnp.where(place == k, index_held[k], numbers)
        numbers_out[...] = numbers
        copies[0].wait()
        valid_out[...] = valid_held[...].astype(jnp.bfloat16)

    vmem, anywhere = pl.BlockSpec(memory_space=pltpu.VMEM), pl.BlockSpec(memory_space=pl.ANY)
    return pl.pallas_call(
        body,
        out_shape=[jax.ShapeDtypeStruct(valid.shape, jnp.bfloat16), jax.ShapeDtypeStruct((stations, rows), jnp.int32)],
        in_specs=[anywhere] * 3,
        out_specs=[vmem] * 2,
        scratch_shapes=[
            pltpu.VMEM(valid.shape, jnp.int32),
            pltpu.SMEM(station_index.shape, jnp.int32),
            pltpu.SemaphoreType.DMA((2,)),
        ],
        compiler_params=pltpu.CompilerParams(vmem_limit_bytes=6 * 2**20),
        cost_estimate=cost(0.3),
    )(station_index, valid, after)


def whiten_rows(raw, others, total_bins):
    part = raw.astype(jnp.float32)
    width = part.shape[1] // 2
    real, imag = part[:, :width], part[:, width:]
    power = real * real + imag * imag + others
    factor = jnp.where(others < 0.0, 0.0, lax.rsqrt(power / total_bins + 1e-05))
    return (real * factor).astype(jnp.bfloat16), (imag * factor).astype(jnp.bfloat16)


def whiten_own(raw, valid, received, total_bins):
    rows, width = valid.shape

    def body(raw_ref, valid_ref, *refs):
        others = sum(ref[...].astype(jnp.float32) for ref in refs[:-2])
        others = jnp.where(valid_ref[...].astype(jnp.float32) > 0.0, others, -1.0).astype(jnp.bfloat16)
        refs[-1][...] = others
        refs[-2][:, :width], refs[-2][:, width:] = whiten_rows(raw_ref[...], others.astype(jnp.float32), total_bins)

    vmem = pl.BlockSpec(memory_space=pltpu.VMEM)
    return pl.pallas_call(
        body,
        out_shape=[jax.ShapeDtypeStruct(raw.shape, jnp.bfloat16), jax.ShapeDtypeStruct((rows, width), jnp.bfloat16)],
        in_specs=[vmem] * (2 + len(received)),
        out_specs=[vmem, vmem],
        compiler_params=pltpu.CompilerParams(vmem_limit_bytes=6 * 2**20),
        cost_estimate=cost(0.2),
    )(raw, valid, *received)


def whiten_passed(raw, others, total_bins):
    width = others.shape[1]

    def body(raw_ref, others_ref, out_ref):
        out_ref[:, :width], out_ref[:, width:] = whiten_rows(raw_ref[...], others_ref[...].astype(jnp.float32), total_bins)

    vmem = pl.BlockSpec(memory_space=pltpu.VMEM)
    return pl.pallas_call(
        body,
        out_shape=jax.ShapeDtypeStruct(raw.shape, jnp.bfloat16),
        in_specs=[vmem, vmem],
        out_specs=vmem,
        compiler_params=pltpu.CompilerParams(vmem_limit_bytes=6 * 2**20),
        cost_estimate=cost(0.2),
    )(raw, others)


def select(numbers, first):
    wanted = numbers - first
    return (wanted == lax.broadcasted_iota(jnp.int32, wanted.shape, 1)).astype(jnp.bfloat16)


def pick(blocks, numbers, places):
    rows, depth = sum(piece.shape[0] for piece in blocks[0]), blocks[0][0].shape[1]
    pieces = [len(block) for block in blocks]

    def body(numbers_ref, *refs):
        picked = None
        for k, place in enumerate(places()[: len(blocks)]):
            first = sum(pieces[:k])
            block = jnp.concatenate([ref[...] for ref in refs[first : first + pieces[k]]], axis=0)
            found = jnp.dot(select(numbers_ref[...], place * rows), block, preferred_element_type=jnp.float32)
            picked = found if picked is None else picked + found
        refs[-1][...] = picked.astype(jnp.bfloat16)

    vmem = pl.BlockSpec(memory_space=pltpu.VMEM)
    return pl.pallas_call(
        body,
        out_shape=jax.ShapeDtypeStruct((numbers.shape[0], depth), jnp.bfloat16),
        in_specs=[vmem] * (1 + sum(pieces)),
        out_specs=vmem,
        compiler_params=pltpu.CompilerParams(vmem_limit_bytes=6 * 2**20),
        cost_estimate=cost(0.1),
    )(numbers, *(piece for block in blocks for piece in block))


def cross_blocks(left, blocks, places, cross, total, scaling, numbers=None, stations=None, microseconds=0.0):
    rows, depth = left.shape[0] // 2, left.shape[1]
    pieces = [len(block) for block in blocks]
    count = sum(pieces)
    vmem, anywhere = pl.BlockSpec(memory_space=pltpu.VMEM), pl.BlockSpec(memory_space=pl.ANY)
    operands = [left, *(piece for block in blocks for piece in block)]
    specs = [vmem] * len(operands)
    for more in (numbers, stations):
        if more is not None:
            operands.append(more)
            specs.append(vmem)
    aliases = {}
    if cross is not None:
        aliases = {len(operands): 0}
        operands.append(cross)
        specs.append(anywhere)
    shapes, out_specs = [jax.ShapeDtypeStruct((2, rows, total), jnp.bfloat16)], [anywhere]
    if numbers is not None:
        shapes.append(jax.ShapeDtypeStruct((numbers.shape[0], depth), jnp.bfloat16))
        out_specs.append(vmem)

    def body(left_ref, *refs):
        held, sems = refs[-2:]
        out_ref = refs[len(operands) - 1]
        copies, picked = [], None
        for k, place in enumerate(places()):
            first = sum(pieces[:k])
            block = jnp.concatenate([ref[...] for ref in refs[first : first + pieces[k]]], axis=0)
            product = lax.dot_general(left_ref[...], block, ROWS_T, preferred_element_type=jnp.float32)
            held[k] = (product * scaling).astype(jnp.bfloat16).reshape(2, rows, rows)
            start = pl.multiple_of(place * rows, rows)
            copies.append(pltpu.make_async_copy(held.at[k], out_ref.at[:, :, pl.ds(start, rows)], sems.at[k]))
            copies[k].start()
            if numbers is not None:
                found = jnp.dot(select(refs[count][...], start), block, preferred_element_type=jnp.float32)
                picked = found if picked is None else picked + found
        if numbers is not None:
            if stations is not None:
                picked = picked + refs[count + 1][...].astype(jnp.float32)
            refs[len(operands)][...] = picked.astype(jnp.bfloat16)
        for copy in copies:
            copy.wait()

    out = pl.pallas_call(
        body,
        out_shape=shapes,
        in_specs=specs,
        out_specs=out_specs,
        scratch_shapes=[
            pltpu.VMEM((len(blocks), 2, rows, rows), jnp.bfloat16),
            pltpu.SemaphoreType.DMA((len(blocks),)),
        ],
        input_output_aliases=aliases,
        compiler_params=pltpu.CompilerParams(vmem_limit_bytes=6 * 2**20),
        cost_estimate=cost(microseconds),
    )(*operands)
    return out if numbers is not None else out[0]


def station_kernel(parts, left, scaling):
    rows, width = left.shape[0] // 2, left.shape[1] // 2
    stations = parts[0].shape[0]

    def body(left_ref, *refs):
        found = sum(ref[...].astype(jnp.float32) for ref in refs[:-1])
        turned = jnp.concatenate([found[:, width:], -found[:, :width]], axis=1)
        both = jnp.concatenate([found, turned], axis=0).astype(jnp.bfloat16)
        refs[-1][...] = lax.dot_general(both, left_ref[:rows, :], ROWS_T, preferred_element_type=jnp.float32) * scaling

    vmem = pl.BlockSpec(memory_space=pltpu.VMEM)
    return pl.pallas_call(
        body,
        out_shape=jax.ShapeDtypeStruct((2 * stations, rows), jnp.float32),
        in_specs=[vmem] * (1 + len(parts)),
        out_specs=vmem,
        compiler_params=pltpu.CompilerParams(vmem_limit_bytes=6 * 2**20),
        cost_estimate=cost(0.2),
    )(left, *parts)


def spread(table, stations):
    parts, lags = table.shape
    high = lax.reduce_precision(table, 8, 7)
    low = table - high
    same = jnp.eye(stations, dtype=jnp.float32)[None, :, :, None]

    def blocks(values):
        return (values[:, None, None, :] * same).reshape(parts * stations, stations * lags).astype(jnp.bfloat16)

    return jnp.concatenate([blocks(high), blocks(low), blocks(high)], axis=0)


def lag_sums(kernels, table):
    rows = kernels[0].shape[1]
    stations = kernels[0].shape[0] // 2
    lags = table.shape[1] // stations
    groups = 4
    each = stations // groups

    def body(table_ref, *refs):
        out_ref, held, sems = refs[-3:]
        parts = jnp.concatenate([ref[...] for ref in refs[:-3]], axis=0)
        high = parts.astype(jnp.bfloat16).astype(jnp.float32)
        columns = jnp.concatenate([high, high, parts - high], axis=0).T.astype(jnp.bfloat16)
        copies = []
        for group in range(groups):
            part = slice(group * each * lags, (group + 1) * each * lags)
            sums = jnp.dot(columns, table_ref[:, part], preferred_element_type=jnp.float32)
            for k in range(each):
                held[group * each + k] = sums[:, k * lags : (k + 1) * lags]
            part = pl.ds(group * each, each)
            copies.append(pltpu.make_async_copy(held.at[part], out_ref.at[part], sems.at[group]))
            copies[group].start()
        for copy in copies:
            copy.wait()

    vmem = pl.BlockSpec(memory_space=pltpu.VMEM)
    return pl.pallas_call(
        body,
        out_shape=jax.ShapeDtypeStruct((stations, rows, lags), jnp.float32),
        in_specs=[vmem] * (1 + len(kernels)),
        out_specs=pl.BlockSpec(memory_space=pl.ANY),
        scratch_shapes=[pltpu.VMEM((stations, rows, lags), jnp.float32), pltpu.SemaphoreType.DMA((groups,))],
        compiler_params=pltpu.CompilerParams(vmem_limit_bytes=8 * 2**20),
        cost_estimate=cost(8.0),
    )(table, *kernels)


def make_on_device(group_size, freq_size):
    chips = group_size // 2
    ring = ring_pairs(group_size)
    across = [
        (device, device_of(place_of(device, chips) - 1 + 2 * (device % 2), 1 - device % 2, chips)) for device in range(group_size)
    ]

    def swap_by(bit):
        return [(g, g ^ bit) for g in range(group_size)]

    def swap_pieces(block, pieces):
        rows = block.shape[0] // pieces
        return [lax.ppermute(block[k * rows : (k + 1) * rows], "grp", swap_by(1)) for k in range(pieces)]

    def swap(block):
        return swap_pieces(block, 2)

    def from_freq(shift):
        return [(f, (f + shift) % freq_size) for f in range(freq_size)]

    def on_device(spectra, valid, station_index):
        bin_count, chan_count, double_width = spectra.shape
        assert bin_count == 1
        window_count = double_width // 2
        freq_index = lax.axis_index("freq")
        total_chans = chan_count * group_size
        total_bins = bin_count * freq_size
        scaling = 1.0 / math.sqrt(window_count)

        station_count = station_index.shape[0]
        lags_here = LAGS // freq_size
        lag_values = (freq_index * lags_here + jnp.arange(lags_here, dtype=jnp.int32)).astype(jnp.float32)
        tables = []
        for shift in range(freq_size):
            bin_value = lax.rem(freq_index - shift + freq_size, freq_size).astype(jnp.float32) + 1.0
            phase = math.pi * bin_value * lag_values / LAGS
            tables += [jnp.cos(phase), -jnp.sin(phase)]
        table = spread(jnp.stack(tables) / math.sqrt(total_bins), station_count)

        raw, power = band_power(spectra[0])
        valid, numbers = prepare(valid, station_index, raw)
        received = [lax.ppermute(power, "freq", from_freq(shift)) for shift in range(1, freq_size)]
        raw_flying = lax.ppermute(raw, "grp", ring)
        raw_sibling = lax.ppermute(raw, "grp", swap_by(1))
        whitened, others = whiten_own(raw, valid, received, total_bins)
        others_flying = lax.ppermute(others, "grp", ring)
        others_sibling = lax.ppermute(others, "grp", swap_by(1))
        swapped = [whiten_passed(raw_sibling, others_sibling, total_bins)]
        flying = [None, lax.ppermute(jnp.concatenate(swapped, axis=0), "grp", ring)]
        left = jnp.concatenate(
            [whitened, jnp.concatenate([whitened[:, window_count:], -whitened[:, :window_count]], axis=1)], axis=0
        )
        flying[0] = whiten_passed(raw_flying, others_flying, total_bins)

        steps = chips - 1
        waiting, ahead, kernels = [], [], []
        cross = stations = None
        for step in range(steps):
            arrived, cross, stations, swapped, ahead, kernels = lax.optimization_barrier(
                (flying[step], cross, stations, swapped, ahead, kernels)
            )
            if step + 2 < steps:
                flying.append(lax.ppermute(arrived, "grp", ring))
            if step + 3 == steps:
                found = pick([[arrived]], numbers, functools.partial(ring_blocks, step, chips))
                ahead = [lax.ppermute(lax.ppermute(found, "grp", swap_by(1)), "grp", across)]
            if step == 2:
                table, cross = lax.optimization_barrier((table, cross))
            if step + 2 == steps:
                ahead.append(lax.ppermute(ahead[0], "grp", swap_by(1)))
            next_swapped = swap(arrived)
            if step == 0:
                cross, stations = cross_blocks(
                    left, [[whitened], swapped], own_blocks, None, total_chans, scaling, numbers, None, 4.0
                )
            elif step + 1 < steps:
                cross, stations = cross_blocks(left, [waiting, swapped], places, cross, total_chans, scaling, numbers, stations)
            waiting, swapped, places = [arrived], next_swapped, functools.partial(ring_blocks, step, chips)
            if step + 2 == steps:
                found = pick([waiting, swapped], numbers, places)
                kernels = [station_kernel([stations, found, *ahead], left, scaling)]
                others = [lax.ppermute(kernels[0], "freq", from_freq(shift)) for shift in range(1, freq_size)]
                cross, kernels = lax.optimization_barrier((cross, kernels))
                cross = cross_blocks(left, [waiting, swapped], places, cross, total_chans, scaling)
        station_gather = lag_sums(kernels + others, table)
        cross = cross_blocks(left, [waiting, swapped], places, cross, total_chans, scaling)
        return (cross[None], station_gather)

    return on_device


def solution(mesh):
    placed = (P("freq", "grp", None), P("grp", None), P())
    return jax.shard_map(
        make_on_device(mesh.shape["grp"], mesh.shape["freq"]),
        mesh=mesh,
        in_specs=placed,
        out_specs=(P("freq", None, "grp", None), P(None, "grp", "freq")),
        check_vma=False,
    )
```

```python
import functools
import math

import jax
import jax.numpy as jnp
from jax import lax
from jax.experimental import pallas as pl
from jax.experimental.pallas import tpu as pltpu
from jax.sharding import PartitionSpec as P

LAGS = 256
ROWS_T = (((1,), (1,)), ((), ()))


def device_of(place, core, chips):
    place %= chips
    z, x = (place, 0) if place < chips // 2 else (chips - 1 - place, 1)
    return z * 4 + x * 2 + core


def place_of(device, chips):
    z, x = device // 4, device // 2 % 2
    return z if x == 0 else chips - 1 - z


def ring_pairs(group_size):
    chips = group_size // 2
    return [
        (device, device_of(place_of(device, chips) + 1 - 2 * (device % 2), device % 2, chips)) for device in range(group_size)
    ]


def block_of(place, core, chips):
    place = lax.rem(place + chips, chips)
    half = chips // 2
    return jnp.where(place < half, place * 4, (chips - 1 - place) * 4 + 2) + core


def own_blocks():
    group_index = lax.axis_index("grp")
    return [group_index, group_index + 1 - 2 * lax.rem(group_index, 2)]


def ring_blocks(step, chips):
    group_index = lax.axis_index("grp")
    core = lax.rem(group_index, 2)
    z, x = group_index // 4, lax.rem(group_index // 2, 2)
    place = jnp.where(x == 0, z, chips - 1 - z)
    back = (step // 2 + 1) * (1 - 2 * core)
    kept = core if step % 2 == 0 else 1 - core
    return [block_of(place - back, kept, chips), block_of(place + back, 1 - kept, chips)]


def cost(microseconds):
    return pl.CostEstimate(flops=int(microseconds * 1.15e9), bytes_accessed=0, transcendentals=0)


def band_power(raw):
    rows, width = raw.shape[0], raw.shape[1] // 2

    def body(raw_ref, raw_out, power_out):
        part = raw_ref[...].astype(jnp.float32)
        power_out[...] = (part[:, :width] * part[:, :width] + part[:, width:] * part[:, width:]).astype(jnp.bfloat16)
        raw_out[...] = raw_ref[...]

    vmem = pl.BlockSpec(memory_space=pltpu.VMEM)
    return pl.pallas_call(
        body,
        out_shape=[jax.ShapeDtypeStruct(raw.shape, jnp.bfloat16), jax.ShapeDtypeStruct((rows, width), jnp.bfloat16)],
        in_specs=[vmem],
        out_specs=[vmem, vmem],
        compiler_params=pltpu.CompilerParams(vmem_limit_bytes=6 * 2**20),
        cost_estimate=cost(0.1),
    )(raw)


def prepare(valid, station_index, after):
    rows, width = valid.shape
    stations = station_index.shape[0]

    def body(index_ref, valid_ref, _, valid_out, numbers_out, valid_held, index_held, sems):
        copies = [
            pltpu.make_async_copy(valid_ref, valid_held, sems.at[0]),
            pltpu.make_async_copy(index_ref, index_held, sems.at[1]),
        ]
        for copy in copies:
            copy.start()
        copies[1].wait()
        place = lax.broadcasted_iota(jnp.int32, (stations, rows), 0)
        numbers = jnp.zeros((stations, rows), jnp.int32)
        for k in range(stations):
            numbers = jnp.where(place == k, index_held[k], numbers)
        numbers_out[...] = numbers
        copies[0].wait()
        valid_out[...] = valid_held[...].astype(jnp.bfloat16)

    vmem, anywhere = pl.BlockSpec(memory_space=pltpu.VMEM), pl.BlockSpec(memory_space=pl.ANY)
    return pl.pallas_call(
        body,
        out_shape=[jax.ShapeDtypeStruct(valid.shape, jnp.bfloat16), jax.ShapeDtypeStruct((stations, rows), jnp.int32)],
        in_specs=[anywhere] * 3,
        out_specs=[vmem] * 2,
        scratch_shapes=[
            pltpu.VMEM(valid.shape, jnp.int32),
            pltpu.SMEM(station_index.shape, jnp.int32),
            pltpu.SemaphoreType.DMA((2,)),
        ],
        compiler_params=pltpu.CompilerParams(vmem_limit_bytes=6 * 2**20),
        cost_estimate=cost(0.3),
    )(station_index, valid, after)


def whiten_rows(raw, others, total_bins):
    part = raw.astype(jnp.float32)
    width = part.shape[1] // 2
    real, imag = part[:, :width], part[:, width:]
    power = real * real + imag * imag + others
    factor = jnp.where(others < 0.0, 0.0, lax.rsqrt(power / total_bins + 1e-05))
    return (real * factor).astype(jnp.bfloat16), (imag * factor).astype(jnp.bfloat16)


def whiten_own(raw, valid, received, total_bins):
    rows, width = valid.shape

    def body(raw_ref, valid_ref, *refs):
        others = sum(ref[...].astype(jnp.float32) for ref in refs[:-2])
        others = jnp.where(valid_ref[...].astype(jnp.float32) > 0.0, others, -1.0).astype(jnp.bfloat16)
        refs[-1][...] = others
        refs[-2][:, :width], refs[-2][:, width:] = whiten_rows(raw_ref[...], others.astype(jnp.float32), total_bins)

    vmem = pl.BlockSpec(memory_space=pltpu.VMEM)
    return pl.pallas_call(
        body,
        out_shape=[jax.ShapeDtypeStruct(raw.shape, jnp.bfloat16), jax.ShapeDtypeStruct((rows, width), jnp.bfloat16)],
        in_specs=[vmem] * (2 + len(received)),
        out_specs=[vmem, vmem],
        compiler_params=pltpu.CompilerParams(vmem_limit_bytes=6 * 2**20),
        cost_estimate=cost(0.2),
    )(raw, valid, *received)


def whiten_passed(raw, others, total_bins):
    width = others.shape[1]

    def body(raw_ref, others_ref, out_ref):
        out_ref[:, :width], out_ref[:, width:] = whiten_rows(raw_ref[...], others_ref[...].astype(jnp.float32), total_bins)

    vmem = pl.BlockSpec(memory_space=pltpu.VMEM)
    return pl.pallas_call(
        body,
        out_shape=jax.ShapeDtypeStruct(raw.shape, jnp.bfloat16),
        in_specs=[vmem, vmem],
        out_specs=vmem,
        compiler_params=pltpu.CompilerParams(vmem_limit_bytes=6 * 2**20),
        cost_estimate=cost(0.2),
    )(raw, others)


def select(numbers, first):
    wanted = numbers - first
    return (wanted == lax.broadcasted_iota(jnp.int32, wanted.shape, 1)).astype(jnp.bfloat16)


def pick(blocks, numbers, places):
    rows, depth = sum(piece.shape[0] for piece in blocks[0]), blocks[0][0].shape[1]
    pieces = [len(block) for block in blocks]

    def body(numbers_ref, *refs):
        picked = None
        for k, place in enumerate(places()[: len(blocks)]):
            first = sum(pieces[:k])
            block = jnp.concatenate([ref[...] for ref in refs[first : first + pieces[k]]], axis=0)
            found = jnp.dot(select(numbers_ref[...], place * rows), block, preferred_element_type=jnp.float32)
            picked = found if picked is None else picked + found
        refs[-1][...] = picked.astype(jnp.bfloat16)

    vmem = pl.BlockSpec(memory_space=pltpu.VMEM)
    return pl.pallas_call(
        body,
        out_shape=jax.ShapeDtypeStruct((numbers.shape[0], depth), jnp.bfloat16),
        in_specs=[vmem] * (1 + sum(pieces)),
        out_specs=vmem,
        compiler_params=pltpu.CompilerParams(vmem_limit_bytes=6 * 2**20),
        cost_estimate=cost(0.1),
    )(numbers, *(piece for block in blocks for piece in block))


def cross_blocks(left, blocks, places, cross, total, scaling, numbers=None, stations=None, microseconds=0.0):
    rows, depth = left.shape[0] // 2, left.shape[1]
    pieces = [len(block) for block in blocks]
    count = sum(pieces)
    vmem, anywhere = pl.BlockSpec(memory_space=pltpu.VMEM), pl.BlockSpec(memory_space=pl.ANY)
    operands = [left, *(piece for block in blocks for piece in block)]
    specs = [vmem] * len(operands)
    for more in (numbers, stations):
        if more is not None:
            operands.append(more)
            specs.append(vmem)
    aliases = {}
    if cross is not None:
        aliases = {len(operands): 0}
        operands.append(cross)
        specs.append(anywhere)
    shapes, out_specs = [jax.ShapeDtypeStruct((2, rows, total), jnp.bfloat16)], [anywhere]
    if numbers is not None:
        shapes.append(jax.ShapeDtypeStruct((numbers.shape[0], depth), jnp.bfloat16))
        out_specs.append(vmem)

    def body(left_ref, *refs):
        held, sems = refs[-2:]
        out_ref = refs[len(operands) - 1]
        copies, picked = [], None
        for k, place in enumerate(places()):
            first = sum(pieces[:k])
            block = jnp.concatenate([ref[...] for ref in refs[first : first + pieces[k]]], axis=0)
            product = lax.dot_general(left_ref[...], block, ROWS_T, preferred_element_type=jnp.float32)
            held[k] = (product * scaling).astype(jnp.bfloat16).reshape(2, rows, rows)
            start = pl.multiple_of(place * rows, rows)
            copies.append(pltpu.make_async_copy(held.at[k], out_ref.at[:, :, pl.ds(start, rows)], sems.at[k]))
            copies[k].start()
            if numbers is not None:
                found = jnp.dot(select(refs[count][...], start), block, preferred_element_type=jnp.float32)
                picked = found if picked is None else picked + found
        if numbers is not None:
            if stations is not None:
                picked = picked + refs[count + 1][...].astype(jnp.float32)
            refs[len(operands)][...] = picked.astype(jnp.bfloat16)
        for copy in copies:
            copy.wait()

    out = pl.pallas_call(
        body,
        out_shape=shapes,
        in_specs=specs,
        out_specs=out_specs,
        scratch_shapes=[
            pltpu.VMEM((len(blocks), 2, rows, rows), jnp.bfloat16),
            pltpu.SemaphoreType.DMA((len(blocks),)),
        ],
        input_output_aliases=aliases,
        compiler_params=pltpu.CompilerParams(vmem_limit_bytes=6 * 2**20),
        cost_estimate=cost(microseconds),
    )(*operands)
    return out if numbers is not None else out[0]


def station_kernel(parts, left, scaling):
    rows, width = left.shape[0] // 2, left.shape[1] // 2
    stations = parts[0].shape[0]

    def body(left_ref, *refs):
        found = sum(ref[...].astype(jnp.float32) for ref in refs[:-1])
        turned = jnp.concatenate([found[:, width:], -found[:, :width]], axis=1)
        both = jnp.concatenate([found, turned], axis=0).astype(jnp.bfloat16)
        refs[-1][...] = lax.dot_general(both, left_ref[:rows, :], ROWS_T, preferred_element_type=jnp.float32) * scaling

    vmem = pl.BlockSpec(memory_space=pltpu.VMEM)
    return pl.pallas_call(
        body,
        out_shape=jax.ShapeDtypeStruct((2 * stations, rows), jnp.float32),
        in_specs=[vmem] * (1 + len(parts)),
        out_specs=vmem,
        compiler_params=pltpu.CompilerParams(vmem_limit_bytes=6 * 2**20),
        cost_estimate=cost(0.2),
    )(left, *parts)


def spread(table, stations):
    parts, lags = table.shape
    high = lax.reduce_precision(table, 8, 7)
    low = table - high
    same = jnp.eye(stations, dtype=jnp.float32)[None, :, :, None]

    def blocks(values):
        return (values[:, None, None, :] * same).reshape(parts * stations, stations * lags).astype(jnp.bfloat16)

    return jnp.concatenate([blocks(high), blocks(low), blocks(high)], axis=0)


def lag_sums(kernels, table):
    rows = kernels[0].shape[1]
    stations = kernels[0].shape[0] // 2
    lags = table.shape[1] // stations
    groups = 4
    each = stations // groups

    def body(table_ref, *refs):
        out_ref, held, sems = refs[-3:]
        parts = jnp.concatenate([ref[...] for ref in refs[:-3]], axis=0)
        high = parts.astype(jnp.bfloat16).astype(jnp.float32)
        columns = jnp.concatenate([high, high, parts - high], axis=0).T.astype(jnp.bfloat16)
        copies = []
        for group in range(groups):
            part = slice(group * each * lags, (group + 1) * each * lags)
            sums = jnp.dot(columns, table_ref[:, part], preferred_element_type=jnp.float32)
            for k in range(each):
                held[group * each + k] = sums[:, k * lags : (k + 1) * lags]
            part = pl.ds(group * each, each)
            copies.append(pltpu.make_async_copy(held.at[part], out_ref.at[part], sems.at[group]))
            copies[group].start()
        for copy in copies:
            copy.wait()

    vmem = pl.BlockSpec(memory_space=pltpu.VMEM)
    return pl.pallas_call(
        body,
        out_shape=jax.ShapeDtypeStruct((stations, rows, lags), jnp.float32),
        in_specs=[vmem] * (1 + len(kernels)),
        out_specs=pl.BlockSpec(memory_space=pl.ANY),
        scratch_shapes=[pltpu.VMEM((stations, rows, lags), jnp.float32), pltpu.SemaphoreType.DMA((groups,))],
        compiler_params=pltpu.CompilerParams(vmem_limit_bytes=8 * 2**20),
        cost_estimate=cost(8.0),
    )(table, *kernels)


def make_on_device(group_size, freq_size):
    chips = group_size // 2
    ring = ring_pairs(group_size)
    across = [
        (device, device_of(place_of(device, chips) - 1 + 2 * (device % 2), 1 - device % 2, chips)) for device in range(group_size)
    ]

    def swap_by(bit):
        return [(g, g ^ bit) for g in range(group_size)]

    def swap_pieces(block, pieces):
        rows = block.shape[0] // pieces
        return [lax.ppermute(block[k * rows : (k + 1) * rows], "grp", swap_by(1)) for k in range(pieces)]

    def swap(block):
        return swap_pieces(block, 2)

    def from_freq(shift):
        return [(f, (f + shift) % freq_size) for f in range(freq_size)]

    def on_device(spectra, valid, station_index):
        bin_count, chan_count, double_width = spectra.shape
        assert bin_count == 1
        window_count = double_width // 2
        freq_index = lax.axis_index("freq")
        total_chans = chan_count * group_size
        total_bins = bin_count * freq_size
        scaling = 1.0 / math.sqrt(window_count)

        station_count = station_index.shape[0]
        lags_here = LAGS // freq_size
        lag_values = (freq_index * lags_here + jnp.arange(lags_here, dtype=jnp.int32)).astype(jnp.float32)
        tables = []
        for shift in range(freq_size):
            bin_value = lax.rem(freq_index - shift + freq_size, freq_size).astype(jnp.float32) + 1.0
            phase = math.pi * bin_value * lag_values / LAGS
            tables += [jnp.cos(phase), -jnp.sin(phase)]
        table = spread(jnp.stack(tables) / math.sqrt(total_bins), station_count)

        raw, power = band_power(spectra[0])
        valid, numbers = prepare(valid, station_index, raw)
        received = [lax.ppermute(power, "freq", from_freq(shift)) for shift in range(1, freq_size)]
        raw_flying = lax.ppermute(raw, "grp", ring)
        raw_sibling = lax.ppermute(raw, "grp", swap_by(1))
        whitened, others = whiten_own(raw, valid, received, total_bins)
        others_flying = lax.ppermute(others, "grp", ring)
        others_sibling = lax.ppermute(others, "grp", swap_by(1))
        swapped = [whiten_passed(raw_sibling, others_sibling, total_bins)]
        flying = [None, lax.ppermute(jnp.concatenate(swapped, axis=0), "grp", ring)]
        left = jnp.concatenate(
            [whitened, jnp.concatenate([whitened[:, window_count:], -whitened[:, :window_count]], axis=1)], axis=0
        )
        cross, stations = cross_blocks(
            left, [[whitened], swapped], own_blocks, None, total_chans, scaling, numbers, None, 4.0
        )
        flying[0] = whiten_passed(raw_flying, others_flying, total_bins)

        steps = chips - 1
        waiting, ahead, kernels = [], [], []
        for step in range(steps):
            arrived, cross, stations, swapped, ahead, kernels = lax.optimization_barrier(
                (flying[step], cross, stations, swapped, ahead, kernels)
            )
            if step + 2 < steps:
                flying.append(lax.ppermute(arrived, "grp", ring))
            if step + 3 == steps:
                found = pick([[arrived]], numbers, functools.partial(ring_blocks, step, chips))
                ahead = [lax.ppermute(lax.ppermute(found, "grp", swap_by(1)), "grp", across)]
            if step == 2:
                table, cross = lax.optimization_barrier((table, cross))
            if step + 2 == steps:
                ahead.append(lax.ppermute(ahead[0], "grp", swap_by(1)))
            next_swapped = swap(arrived)
            if waiting and step + 1 < steps:
                cross, stations = cross_blocks(left, [waiting, swapped], places, cross, total_chans, scaling, numbers, stations)
            waiting, swapped, places = [arrived], next_swapped, functools.partial(ring_blocks, step, chips)
            if step + 2 == steps:
                found = pick([waiting, swapped], numbers, places)
                kernels = [station_kernel([stations, found, *ahead], left, scaling)]
                others = [lax.ppermute(kernels[0], "freq", from_freq(shift)) for shift in range(1, freq_size)]
                cross, kernels = lax.optimization_barrier((cross, kernels))
                cross = cross_blocks(left, [waiting, swapped], places, cross, total_chans, scaling)
        station_gather = lag_sums(kernels + others, table)
        cross = cross_blocks(left, [waiting, swapped], places, cross, total_chans, scaling)
        return (cross[None], station_gather)

    return on_device


def solution(mesh):
    placed = (P("freq", "grp", None), P("grp", None), P())
    return jax.shard_map(
        make_on_device(mesh.shape["grp"], mesh.shape["freq"]),
        mesh=mesh,
        in_specs=placed,
        out_specs=(P("freq", None, "grp", None), P(None, "grp", "freq")),
        check_vma=False,
    )
```
